128 devices in a mesh: blk: 32 (over z, x, y_lo), grp: 4 (over y_hi, core).
Axes of the slice: x: 4, y: 4 (y_hi: 2, y_lo: 2; y = y_hi * 2 + y_lo), z: 4, core: 2. Of those that a mesh axis runs over, the one named last changes fastest.
Arguments:
- queries: bfloat16 [2048, 2048], P(('blk', 'grp')), may hold values from -0.125 to 0.125
- training: bfloat16 [131072, 2048], P(('blk', 'grp')), may hold values from -24 to 24
Outputs:
- scores: float32 [2048, 131072], P(None, ('blk', 'grp'))
- gram: float32 [2048, 2048], P(('blk', 'grp'))
The draws below stay inside these ranges and needn't reach their ends.
All inputs are finite; a program needn't handle non-finite values.
Results may differ from the reference program's by a relative error of at most 0.0003.
Values may be sent and summed in bfloat16 or wider, within the bound.
A program may use at most 128 MiB of HBM per device.

```python
import jax
import jax.numpy as jnp

K = 2048
TRAIN = 131072
NQ = 2048


def spiked(entries, own_key, source, target, parts, factor):
    owner, partner = [(jnp.arange(entries.shape[dim]) // (entries.shape[dim] // parts)).reshape([-1 if axis == dim else 1 for axis in range(entries.ndim)]) for dim in (source, target)]
    chosen = jax.random.permutation(own_key, parts)[partner]
    strong = (owner == chosen) | (owner == (partner + parts // 2) % parts)
    return jnp.where(strong, factor * entries, entries)


def shard_levels(own_key, shape, pieces, least, largest):
    gain = 1.0
    for position, shards_of in pieces:
        steps = jax.random.uniform(jax.random.fold_in(jax.random.fold_in(own_key, 6), position), (shards_of,), jnp.float32, least / len(pieces), largest / len(pieces))
        gain = gain * jnp.repeat(jnp.exp(steps), shape[position] // shards_of).reshape((-1,) + (1,) * (len(shape) - 1 - position))
    return gain


def gaussian(own_key, dims, scale, limit, pieces=(), held_as=jnp.bfloat16):
    drawn = jax.random.normal(own_key, dims, jnp.float32) * scale
    if len(pieces) > 0:
        drawn = shard_levels(own_key, dims, pieces, -0.22, 0.18) * drawn
    return jnp.clip(drawn, min=-limit, max=limit).astype(held_as)


def bell_draw_with(rng, extent, width, most, cuts, heavy, dtype=jnp.bfloat16):
    result = width * jax.random.normal(rng, extent, jnp.float32)
    if cuts:
        result = result * shard_levels(rng, extent, cuts, -0.22, 0.18)
    return jnp.clip(spiked(result, jax.random.fold_in(rng, 3), *heavy), -most, most).astype(dtype)


def setup_inputs(seed: int = 0) -> dict:
    splits = jax.random.split(jax.random.key(seed), 3)
    queries = gaussian(splits[0], (NQ, K), K ** -0.5, 0.125, ((0, 128),))
    training = bell_draw_with(splits[1], (TRAIN, K), 1.0, 24.0, ((0, 128),), (0, 1, 128, 5.5))
    return {"queries": queries, "training": training}


def reference(queries, training):
    scores = jnp.dot(queries, training.T, preferred_element_type=jnp.float32)
    gram = jnp.dot(training.T, training, preferred_element_type=jnp.float32) * (1.0 / TRAIN)
    return scores, gram
```

```python
import functools

import jax
import jax.numpy as jnp
from jax import lax
from jax.experimental import pallas as pl
from jax.experimental.pallas import tpu as pltpu
from jax.sharding import PartitionSpec as P

MESH = pl.DeviceIdType.MESH
ALL = pl.ds(0, 4)
AXES = ("z", "x", "y")
B = 128
CH = 136
AG_PARTS = (((0, 640), "yxz"), ((640, 1280), "zyx"), ((1280, 2048), "xzy"))
RS_PARTS = (((0, 48), "zxy"), ((48, 96), "xyz"), ((96, 136), "yzx"))
N_SEM = 160


def stored(axis, i):
    return lax.rem(i, 2) * 2 + lax.div(i, 2) if axis == "y" else i


class Net:
    def __init__(self, ssem, rsem):
        blk, grp = lax.axis_index("blk"), lax.axis_index("grp")
        self.at = {
            "z": lax.div(blk, 8),
            "x": lax.rem(lax.div(blk, 2), 4),
            "y": lax.div(grp, 2) * 2 + lax.rem(blk, 2),
        }
        self.core = lax.rem(grp, 2)
        self.group = lax.div(blk, 2)
        self.k = lax.rem(blk, 2) * 4 + grp
        self.ssem, self.rsem = ssem, rsem
        self.count = 0
        self.sent = []

    def device(self, core=None, **moved):
        at = {**self.at, **moved}
        core = self.core if core is None else core
        return (at["z"] * 8 + at["x"] * 2 + lax.rem(at["y"], 2), lax.div(at["y"], 2) * 2 + core)

    def hop(self, axis, by):
        return lax.rem(self.at[axis] + by + 4, 4)

    def neighbour(self, axis, by):
        return self.device(**{axis: self.hop(axis, by)})

    def sibling(self):
        return self.device(core=1 - self.core)

    def send(self, src, dst, to):
        t = self.count
        self.count += 1
        copy = pltpu.make_async_remote_copy(
            src_ref=src,
            dst_ref=dst,
            send_sem=self.ssem.at[t],
            recv_sem=self.rsem.at[t],
            device_id=to,
            device_id_type=MESH,
        )
        copy.start()
        self.sent.append(copy)
        return copy


def member(group, k):
    return (group * 2 + lax.div(k, 4), lax.rem(k, 4))


def gather_part(net, q, cols, order):
    lo, hi = cols

    def region(idx, c=None):
        at = [idx[a] for a in AXES]
        return q.at[at[0], at[1], at[2], net.core, :, pl.ds(lo, hi - lo)] if c is None else q.at[
            at[0], at[1], at[2], net.core, :, pl.ds(*c)
        ]

    def halves(idx):
        free = [a for a in AXES if isinstance(idx[a], pl.Slice)]
        if free:
            return [region({**idx, free[0]: pl.ds(2 * h, 2)}) for h in range(2)]
        mid = (hi - lo) // 256 * 128
        return [region(idx, (lo, mid)), region(idx, (lo + mid, hi - lo - mid))]

    idx = {a: stored(a, net.at[a]) for a in AXES}
    to_sibling = []
    to_sibling.append(net.send(region(idx), region(idx), net.sibling()))
    for axis in order:
        here = region(idx)
        up = net.send(here, here, net.neighbour(axis, 1))
        down = net.send(here, here, net.neighbour(axis, -1))
        from_low = {**idx, axis: stored(axis, net.hop(axis, -1))}
        from_high = {**idx, axis: stored(axis, net.hop(axis, 1))}
        far = {**idx, axis: stored(axis, net.hop(axis, 2))}
        yield
        up.wait_recv()
        src = halves(from_low)[0]
        on_up = net.send(src, src, net.neighbour(axis, 1))
        to_sibling.append(net.send(region(from_low), region(from_low), net.sibling()))
        down.wait_recv()
        src = halves(from_high)[1]
        on_down = net.send(src, src, net.neighbour(axis, -1))
        to_sibling.append(net.send(region(from_high), region(from_high), net.sibling()))
        yield
        on_up.wait_recv()
        on_down.wait_recv()
        to_sibling.append(net.send(region(far), region(far), net.sibling()))
        idx = {**idx, axis: ALL}
    yield
    for copy in to_sibling:
        copy.wait_recv()


def reduce_part(net, p, bufs, rows, order):
    lo, hi = rows

    def region(idx, r=None):
        at = [idx[a] for a in AXES]
        r = (lo, hi - lo) if r is None else r
        return p.at[at[0], at[1], at[2], net.core, pl.ds(*r)]

    def halves(idx):
        free = [a for a in AXES if isinstance(idx[a], pl.Slice)]
        if free:
            return [region({**idx, free[0]: pl.ds(2 * h, 2)}) for h in range(2)]
        mid = (hi - lo + 8) // 16 * 8
        return [region(idx, (lo, mid)), region(idx, (lo + mid, hi - lo - mid))]

    idx = {a: ALL for a in AXES}
    for axis, buf in zip(order, bufs, strict=True):
        far = halves({**idx, axis: stored(axis, net.hop(axis, 2))})
        high = halves({**idx, axis: stored(axis, net.hop(axis, 1))})
        low = halves({**idx, axis: stored(axis, net.hop(axis, -1))})
        idx = {**idx, axis: stored(axis, net.at[axis])}
        mine = halves(idx)
        up, down = net.neighbour(axis, 1), net.neighbour(axis, -1)
        via_up = net.send(far[0], buf[0], up)
        via_down = net.send(far[1], buf[1], down)
        own_up = net.send(high[1], buf[2], up)
        own_down = net.send(low[0], buf[3], down)
        yield
        via_up.wait_recv()
        high[0][...] += buf[0][...]
        sum_up = net.send(high[0], buf[4], up)
        via_down.wait_recv()
        low[1][...] += buf[1][...]
        sum_down = net.send(low[1], buf[5], down)
        yield
        own_up.wait_recv()
        sum_down.wait_recv()
        mine[1][...] += buf[2][...] + buf[5][...]
        own_down.wait_recv()
        sum_up.wait_recv()
        mine[0][...] += buf[3][...] + buf[4][...]


def part_buffers(rows):
    lo, hi = rows
    n = hi - lo
    mid = (n + 8) // 16 * 8
    shapes = []
    for lead in ((2, 4), (2,)):
        shapes.append([lead + (n, B)] * 6)
    shapes.append([(h, B) for h in (mid, n - mid, n - mid, mid, mid, n - mid)])
    return shapes


def step_all(gens):
    left = False
    for g in list(gens):
        try:
            next(g)
            left = True
        except StopIteration:
            gens.remove(g)
    return left


def kernel(scale, *refs):
    (q_in, t_in, s_out, g_out, q, t, p, d2d, s, x, slots) = refs[:11]
    n_rs = 18 * len(RS_PARTS)
    flat = refs[11 : 11 + n_rs]
    ssem, rsem, xsem, lsem = refs[11 + n_rs :]
    bufs = [
        [flat[18 * i + 6 * j : 18 * i + 6 * j + 6] for j in range(3)] for i in range(len(RS_PARTS))
    ]
    net = Net(ssem, rsem)
    zi, xi, yi = (stored(a, net.at[a]) for a in AXES)
    core, group, k = net.core, net.group, net.k
    reach = jnp.where(k == 0, 8, k)
    other = lax.rem(group + reach, 16)

    load_q = pltpu.make_async_copy(q_in, q.at[zi, xi, yi, core], lsem.at[0])
    load_q.start()
    load_t = pltpu.make_async_copy(t_in, t, lsem.at[1])
    load_t.start()

    barrier = pltpu.get_barrier_semaphore()

    def greet(device):
        pl.semaphore_signal(barrier, inc=1, device_id=device, device_id_type=MESH)

    for axis in AXES:
        greet(net.neighbour(axis, 1))
        greet(net.neighbour(axis, -1))
    greet(net.sibling())
    for m in range(1, 8):
        greet(member(group, lax.rem(k + m, 8)))
        greet(member(lax.rem(group + 16 - m, 16), jnp.int32(m)))
    greet(member(lax.rem(group + 8, 16), jnp.int32(0)))
    pl.semaphore_wait(barrier, 22)

    load_q.wait()
    gather = [gather_part(net, q, *part) for part in AG_PARTS]
    step_all(gather)
    load_t.wait()

    p[:, :, :, :, pl.ds(B, 8)] = jnp.zeros((4, 4, 4, 2, 8, B), jnp.float32)
    row = lax.broadcasted_iota(jnp.int32, (B, B), 0)
    col = lax.broadcasted_iota(jnp.int32, (B, B), 1)

    def chunk(g, kk):
        return p.at[lax.div(g, 4), lax.rem(g, 4), kk // 2, kk % 2]

    def strip(i):
        left = t[:, pl.ds(pl.multiple_of(i * 256, 256), 256)]
        for j in range(5):
            jj = lax.rem(i + j, 8)
            right = t[:, pl.ds(pl.multiple_of(jj * 256, 256), 256)]
            prod = lax.dot_general(
                left, right, (((0,), (0,)), ((), ())), preferred_element_type=jnp.float32
            )
            for r in range(2):
                for c in range(2):
                    block = prod[r * B : r * B + B, c * B : c * B + B]
                    kk = 2 * j + c - r
                    g = 2 * i + r
                    if 1 <= kk <= 7:
                        chunk(g, kk)[pl.ds(0, B), :] = block
                    elif kk == 8:

                        @pl.when(i < 4)
                        def _(block=block, g=g):
                            chunk(g, 0)[pl.ds(0, B), :] = block

                    elif kk == 0:

                        @pl.when(i < 4)
                        def _(block=block, g=g):
                            chunk(g + 8, 0)[pl.ds(0, B), :] = block

                        @pl.when(i >= 4)
                        def _(block=block, g=g):
                            here = chunk(g, 0)
                            here[pl.ds(0, B), :] = jnp.where(row <= col, here[pl.ds(0, B), :], block)
                            here[pl.ds(B, 1), :] = jnp.sum(
                                jnp.where(row == col, block, 0.0), axis=0, keepdims=True
                            )

    to_sibling = []
    for z in range(4):
        pl.loop(2 * z, 2 * z + 2)(strip)
        to_sibling.append(net.send(p.at[z, :, :, 1 - core], d2d.at[z], net.sibling()))
        step_all(gather)
    for z in range(4):
        to_sibling[z].wait_recv()

        @pl.loop(0, 4)
        def _(i, z=z):
            p[z, i, :, core] += d2d[z, i]

    reduce = [
        reduce_part(net, p, bufs[i], *part) for i, part in enumerate(RS_PARTS)
    ]
    step_all(reduce)
    while gather:
        step_all(gather)

    stores = []
    for z in range(4):

        @pl.loop(0, 4)
        def _(n, z=z):
            rows = pl.ds(pl.multiple_of(n * 256, 256), 256)
            s[pl.ds(512 * z, 512), rows] = lax.dot_general(
                q[z].reshape(512, 2048),
                t[rows, :],
                (((1,), (1,)), ((), ())),
                preferred_element_type=jnp.float32,
            )

        store = pltpu.make_async_copy(
            s.at[pl.ds(512 * z, 512)], s_out.at[pl.ds(512 * z, 512)], lsem.at[2 + z]
        )
        store.start()
        stores.append(store)
        step_all(reduce)
    while reduce:
        step_all(reduce)

    mine = p[zi, xi, yi, core, pl.ds(0, B), :] * scale
    turned = mine.T
    diagonal = p[zi, xi, yi, core, pl.ds(B, 1), :] * scale
    packed = jnp.logical_and(k == 0, group >= 8)
    first = jnp.where(row <= col, mine, turned)
    second = jnp.where(row > col, mine, jnp.where(row < col, turned, jnp.broadcast_to(diagonal, (B, B))))
    x[0] = jnp.where(packed, second, mine).reshape(8, 16, B)
    x[1] = jnp.where(packed, first, turned).reshape(8, 16, B)
    own_slot = jnp.where(packed, group, other)
    other_slot = jnp.where(packed, other, group)
    slots[own_slot] = x[0, k]
    last = []
    for m in range(1, 8):
        to = lax.rem(k + m, 8)
        copy = pltpu.make_async_remote_copy(
            src_ref=x.at[0, to],
            dst_ref=slots.at[own_slot],
            send_sem=xsem.at[0, m],
            recv_sem=xsem.at[1, m],
            device_id=member(group, to),
            device_id_type=MESH,
        )
        copy.start()
        last.append(copy)
    for m in range(8):
        copy = pltpu.make_async_remote_copy(
            src_ref=x.at[1, m],
            dst_ref=slots.at[other_slot],
            send_sem=xsem.at[0, 8 + m],
            recv_sem=xsem.at[1, 8 + k],
            device_id=member(other, jnp.int32(m)),
            device_id_type=MESH,
        )
        copy.start()
        last.append(copy)
    for m in range(1, 16):
        pltpu.make_async_remote_copy(
            src_ref=x.at[0, 0],
            dst_ref=slots.at[0],
            send_sem=xsem.at[0, m],
            recv_sem=xsem.at[1, m],
            device_id=net.sibling(),
            device_id_type=MESH,
        ).wait_recv()
    g_out[...] = slots[...]
    for copy in last + net.sent:
        copy.wait_send()
    for store in stores:
        store.wait()


def local(scale, queries, training):
    n_rows, width = training.shape
    f32, bf16 = jnp.float32, jnp.bfloat16
    scratch = [
        pltpu.VMEM((4, 4, 4, 2, 16, width), bf16),
        pltpu.VMEM((n_rows, width), bf16),
        pltpu.VMEM((4, 4, 4, 2, CH, B), f32),
        pltpu.VMEM((4, 4, 4, CH, B), f32),
        pltpu.VMEM((2048, n_rows), f32),
        pltpu.VMEM((2, 8, 16, B), f32),
        pltpu.VMEM((16, 16, B), f32),
    ]
    for rows, _ in RS_PARTS:
        for shapes in part_buffers(rows):
            scratch += [pltpu.VMEM(shape, f32) for shape in shapes]
    scratch += [
        pltpu.SemaphoreType.DMA((N_SEM,)),
        pltpu.SemaphoreType.DMA((N_SEM,)),
        pltpu.SemaphoreType.DMA((2, 16)),
        pltpu.SemaphoreType.DMA((6,)),
    ]
    scores, slots = pl.pallas_call(
        functools.partial(kernel, scale),
        out_shape=(
            jax.ShapeDtypeStruct((2048, n_rows), f32),
            jax.ShapeDtypeStruct((16, 16, B), f32),
        ),
        in_specs=[pl.BlockSpec(memory_space=pl.ANY)] * 2,
        out_specs=(
            pl.BlockSpec(memory_space=pl.ANY),
            pl.BlockSpec(memory_space=pltpu.VMEM),
        ),
        scratch_shapes=scratch,
        compiler_params=pltpu.CompilerParams(
            collective_id=0, has_side_effects=True, vmem_limit_bytes=60 * 2**20
        ),
        cost_estimate=pl.CostEstimate(
            flops=2 * 2048 * n_rows * 2048 * 2, bytes_accessed=20 * 2**20, transcendentals=0
        ),
    )(queries, training)
    return scores, slots.transpose(1, 0, 2).reshape(16, 2048)


def solution(mesh):
    in_specs = (P(("blk", "grp"), None), P(("blk", "grp"), None))
    out_specs = (P(None, ("blk", "grp")), P(("blk", "grp"), None))
    return jax.shard_map(
        functools.partial(local, 1.0 / 131072),
        mesh=mesh,
        in_specs=in_specs,
        out_specs=out_specs,
        check_vma=False,
    )
```

```python
import functools

import jax
import jax.numpy as jnp
from jax import lax
from jax.experimental import pallas as pl
from jax.experimental.pallas import tpu as pltpu
from jax.sharding import PartitionSpec as P

MESH = pl.DeviceIdType.MESH
ALL = pl.ds(0, 4)
AXES = ("z", "x", "y")
B = 128
CH = 136
AG_PARTS = (((0, 640), "yxz"), ((640, 1280), "zyx"), ((1280, 2048), "xzy"))
RS_PARTS = (((0, 48), "zxy"), ((48, 96), "xyz"), ((96, 136), "yzx"))
N_SEM = 160
ORDER = (
    "gather",
    "share 0",
    "gram 1",
    "share 1",
    "gram 2",
    "share 2",
    "gather",
    "gram 3",
    "share 3",
    "join 0",
    "join 1",
    "join 2",
    "join 3",
    "reduce",
    "gather",
    "reduce",
    "gather",
    "gather",
    "reduce",
    "gather",
    "scores 0",
    "reduce",
    "scores 1",
    "reduce",
    "scores 2",
    "exchange",
    "scores 3",
)


def stored(axis, i):
    return lax.rem(i, 2) * 2 + lax.div(i, 2) if axis == "y" else i


class Net:
    def __init__(self, ssem, rsem):
        blk, grp = lax.axis_index("blk"), lax.axis_index("grp")
        self.at = {
            "z": lax.div(blk, 8),
            "x": lax.rem(lax.div(blk, 2), 4),
            "y": lax.div(grp, 2) * 2 + lax.rem(blk, 2),
        }
        self.core = lax.rem(grp, 2)
        self.group = lax.div(blk, 2)
        self.k = lax.rem(blk, 2) * 4 + grp
        self.ssem, self.rsem = ssem, rsem
        self.count = 0
        self.sent = []

    def device(self, core=None, **moved):
        at = {**self.at, **moved}
        core = self.core if core is None else core
        return (at["z"] * 8 + at["x"] * 2 + lax.rem(at["y"], 2), lax.div(at["y"], 2) * 2 + core)

    def hop(self, axis, by):
        return lax.rem(self.at[axis] + by + 4, 4)

    def neighbour(self, axis, by):
        return self.device(**{axis: self.hop(axis, by)})

    def sibling(self):
        return self.device(core=1 - self.core)

    def send(self, src, dst, to):
        t = self.count
        self.count += 1
        copy = pltpu.make_async_remote_copy(
            src_ref=src,
            dst_ref=dst,
            send_sem=self.ssem.at[t],
            recv_sem=self.rsem.at[t],
            device_id=to,
            device_id_type=MESH,
        )
        copy.start()
        self.sent.append(copy)
        return copy


def member(group, k):
    return (group * 2 + lax.div(k, 4), lax.rem(k, 4))


def gather_part(net, q, cols, order):
    lo, hi = cols

    def region(idx, c=None):
        at = [idx[a] for a in AXES]
        return q.at[at[0], at[1], at[2], net.core, :, pl.ds(lo, hi - lo)] if c is None else q.at[
            at[0], at[1], at[2], net.core, :, pl.ds(*c)
        ]

    def halves(idx):
        free = [a for a in AXES if isinstance(idx[a], pl.Slice)]
        if free:
            return [region({**idx, free[0]: pl.ds(2 * h, 2)}) for h in range(2)]
        mid = (hi - lo) // 256 * 128
        return [region(idx, (lo, mid)), region(idx, (lo + mid, hi - lo - mid))]

    idx = {a: stored(a, net.at[a]) for a in AXES}
    to_sibling = []
    for step, axis in enumerate(order[:2]):
        here = region(idx)
        copies = [net.send(here, here, net.neighbour(axis, by)) for by in (2, 1, -1)]
        if step == 1:
            to_sibling.append(net.send(here, here, net.sibling()))
        yield
        for copy in copies:
            copy.wait_recv()
        if step == 1:
            for by in (2, 1, -1):
                there = region({**idx, axis: stored(axis, net.hop(axis, by))})
                to_sibling.append(net.send(there, there, net.sibling()))
        idx = {**idx, axis: ALL}
    axis = order[2]
    here = region(idx)
    up = net.send(here, here, net.neighbour(axis, 1))
    down = net.send(here, here, net.neighbour(axis, -1))
    from_low = {**idx, axis: stored(axis, net.hop(axis, -1))}
    from_high = {**idx, axis: stored(axis, net.hop(axis, 1))}
    far = {**idx, axis: stored(axis, net.hop(axis, 2))}
    yield
    up.wait_recv()
    src = halves(from_low)[0]
    on_up = net.send(src, src, net.neighbour(axis, 1))
    down.wait_recv()
    src = halves(from_high)[1]
    on_down = net.send(src, src, net.neighbour(axis, -1))
    to_sibling.append(net.send(region(from_low), region(from_low), net.sibling()))
    to_sibling.append(net.send(region(from_high), region(from_high), net.sibling()))
    yield
    on_up.wait_recv()
    on_down.wait_recv()
    to_sibling.append(net.send(region(far), region(far), net.sibling()))
    yield
    for copy in to_sibling:
        copy.wait_recv()


def reduce_part(net, p, bufs, rows, order):
    lo, hi = rows

    def region(idx, r=None):
        at = [idx[a] for a in AXES]
        r = (lo, hi - lo) if r is None else r
        return p.at[at[0], at[1], at[2], net.core, pl.ds(*r)]

    def halves(idx):
        free = [a for a in AXES if isinstance(idx[a], pl.Slice)]
        if free:
            return [region({**idx, free[0]: pl.ds(2 * h, 2)}) for h in range(2)]
        mid = (hi - lo + 8) // 16 * 8
        return [region(idx, (lo, mid)), region(idx, (lo + mid, hi - lo - mid))]

    idx = {a: ALL for a in AXES}
    axis, buf = order[0], bufs[0]
    far = halves({**idx, axis: stored(axis, net.hop(axis, 2))})
    high = halves({**idx, axis: stored(axis, net.hop(axis, 1))})
    low = halves({**idx, axis: stored(axis, net.hop(axis, -1))})
    idx = {**idx, axis: stored(axis, net.at[axis])}
    mine = halves(idx)
    up, down = net.neighbour(axis, 1), net.neighbour(axis, -1)
    via_up = net.send(far[0], buf[0], up)
    via_down = net.send(far[1], buf[1], down)
    own_up = net.send(high[1], buf[2], up)
    own_down = net.send(low[0], buf[3], down)
    yield
    via_up.wait_recv()
    high[0][...] += buf[0][...]
    sum_up = net.send(high[0], buf[4], up)
    via_down.wait_recv()
    low[1][...] += buf[1][...]
    sum_down = net.send(low[1], buf[5], down)
    yield
    own_up.wait_recv()
    own_down.wait_recv()
    sum_down.wait_recv()
    mine[1][...] += buf[2][...] + buf[5][...]
    sum_up.wait_recv()
    mine[0][...] += buf[3][...] + buf[4][...]
    for axis, buf in zip(order[1:], bufs[1:], strict=True):
        copies = [
            net.send(region({**idx, axis: stored(axis, net.hop(axis, by))}), buf[i], net.neighbour(axis, by))
            for i, by in enumerate((2, 1, -1))
        ]
        idx = {**idx, axis: stored(axis, net.at[axis])}
        yield
        for copy in copies:
            copy.wait_recv()
        region(idx)[...] += buf[0][...] + buf[1][...] + buf[2][...]


def part_buffers(rows):
    n = rows[1] - rows[0]
    return [[(2, 4, n, B)] * 6, [(4, n, B)] * 3, [(n, B)] * 3]


def step_all(gens):
    left = False
    for g in list(gens):
        try:
            next(g)
            left = True
        except StopIteration:
            gens.remove(g)
    return left


def kernel(scale, *refs):
    (q_in, t_in, s, g_out, q, t, p, d2d, x, slots) = refs[:10]
    *flat, ssem, rsem, xsem, lsem = refs[10:]
    flat = iter(flat)
    bufs = [[[next(flat) for _ in shapes] for shapes in part_buffers(rows)] for rows, _ in RS_PARTS]
    net = Net(ssem, rsem)
    zi, xi, yi = (stored(a, net.at[a]) for a in AXES)
    core, group, k = net.core, net.group, net.k
    reach = jnp.where(k == 0, 8, k)
    other = lax.rem(group + reach, 16)

    load_q = pltpu.make_async_copy(q_in, q.at[zi, xi, yi, core], lsem.at[0])
    load_q.start()
    load_t = pltpu.make_async_copy(t_in, t, lsem.at[1])
    load_t.start()

    barrier = pltpu.get_barrier_semaphore()

    def greet(device):
        pl.semaphore_signal(barrier, inc=1, device_id=device, device_id_type=MESH)

    for axis in AXES:
        greet(net.neighbour(axis, 1))
        greet(net.neighbour(axis, -1))
        greet(net.neighbour(axis, 2))
    greet(net.sibling())
    load_t.wait()

    p[:, :, :, :, pl.ds(B, 8)] = jnp.zeros((4, 4, 4, 2, 8, B), jnp.float32)
    row = lax.broadcasted_iota(jnp.int32, (B, B), 0)
    col = lax.broadcasted_iota(jnp.int32, (B, B), 1)

    def chunk(g, kk):
        return p.at[lax.div(g, 4), lax.rem(g, 4), kk // 2, kk % 2]

    def strip(i):
        left = t[:, pl.ds(pl.multiple_of(i * 256, 256), 256)]
        for j in range(5):
            jj = lax.rem(i + j, 8)
            right = t[:, pl.ds(pl.multiple_of(jj * 256, 256), 256)]
            prod = lax.dot_general(
                left, right, (((0,), (0,)), ((), ())), preferred_element_type=jnp.float32
            )
            for r in range(2):
                for c in range(2):
                    block = prod[r * B : r * B + B, c * B : c * B + B]
                    kk = 2 * j + c - r
                    g = 2 * i + r
                    if 1 <= kk <= 7:
                        chunk(g, kk)[pl.ds(0, B), :] = block
                    elif kk == 8:

                        @pl.when(i < 4)
                        def _(block=block, g=g):
                            chunk(g, 0)[pl.ds(0, B), :] = block

                    elif kk == 0:

                        @pl.when(i < 4)
                        def _(block=block, g=g):
                            chunk(g + 8, 0)[pl.ds(0, B), :] = block

                        @pl.when(i >= 4)
                        def _(block=block, g=g):
                            here = chunk(g, 0)
                            here[pl.ds(0, B), :] = jnp.where(row <= col, here[pl.ds(0, B), :], block)
                            here[pl.ds(B, 1), :] = jnp.sum(
                                jnp.where(row == col, block, 0.0), axis=0, keepdims=True
                            )

    to_sibling = []

    def gram_rows(z):
        pl.loop(2 * z, 2 * z + 2)(strip)

    def share(z):
        to_sibling.append(net.send(p.at[z, :, :, 1 - core], d2d.at[z], net.sibling()))

    def join(z):
        to_sibling[z].wait_recv()

        @pl.loop(0, 4)
        def _(i):
            p[z, i, :, core] += d2d[z, i]

    def scores(z):
        s[pl.ds(512 * z, 512), :] = lax.dot_general(
            q[z].reshape(512, 2048),
            t[...],
            (((1,), (1,)), ((), ())),
            preferred_element_type=jnp.float32,
        )

    last = []

    def exchange(_):
        mine = p[zi, xi, yi, core, pl.ds(0, B), :] * scale
        turned = mine.T
        diagonal = p[zi, xi, yi, core, pl.ds(B, 1), :] * scale
        packed = jnp.logical_and(k == 0, group >= 8)
        first = jnp.where(row <= col, mine, turned)
        second = jnp.where(row > col, mine, jnp.where(row < col, turned, jnp.broadcast_to(diagonal, (B, B))))
        x[0] = jnp.where(packed, second, mine).reshape(8, 16, B)
        x[1] = jnp.where(packed, first, turned).reshape(8, 16, B)
        own_slot = jnp.where(packed, group, other)
        other_slot = jnp.where(packed, other, group)
        slots[own_slot] = x[0, k]
        for m in range(1, 8):
            to = lax.rem(k + m, 8)
            copy = pltpu.make_async_remote_copy(
                src_ref=x.at[0, to],
                dst_ref=slots.at[own_slot],
                send_sem=xsem.at[0, m],
                recv_sem=xsem.at[1, m],
                device_id=member(group, to),
                device_id_type=MESH,
            )
            copy.start()
            last.append(copy)
        for m in range(8):
            copy = pltpu.make_async_remote_copy(
                src_ref=x.at[1, m],
                dst_ref=slots.at[other_slot],
                send_sem=xsem.at[0, 8 + m],
                recv_sem=xsem.at[1, 8 + k],
                device_id=member(other, jnp.int32(m)),
                device_id_type=MESH,
            )
            copy.start()
            last.append(copy)

    gather = [gather_part(net, q, *part) for part in AG_PARTS]
    reduce = [reduce_part(net, p, bufs[i], *part) for i, part in enumerate(RS_PARTS)]
    plan = {
        "gather": lambda _: step_all(gather),
        "reduce": lambda _: step_all(reduce),
        "gram": gram_rows,
        "share": share,
        "join": join,
        "scores": scores,
        "exchange": exchange,
    }

    gram_rows(0)
    pl.semaphore_wait(barrier, 10)
    load_q.wait()
    for step in ORDER:
        name, *at = step.split()
        plan[name](int(at[0]) if at else None)
    assert not step_all(gather) and not step_all(reduce)

    for m in range(1, 16):
        pltpu.make_async_remote_copy(
            src_ref=x.at[0, 0],
            dst_ref=slots.at[0],
            send_sem=xsem.at[0, m],
            recv_sem=xsem.at[1, m],
            device_id=net.sibling(),
            device_id_type=MESH,
        ).wait_recv()
    for c in range(16):
        g_out[:, pl.ds(c * B, B)] = slots[c]
    for copy in last + net.sent:
        copy.wait_send()


def local(scale, queries, training):
    n_rows, width = training.shape
    f32, bf16 = jnp.float32, jnp.bfloat16
    scratch = [
        pltpu.VMEM((4, 4, 4, 2, 16, width), bf16),
        pltpu.VMEM((n_rows, width), bf16),
        pltpu.VMEM((4, 4, 4, 2, CH, B), f32),
        pltpu.VMEM((4, 4, 4, CH, B), f32),
        pltpu.VMEM((2, 8, 16, B), f32),
        pltpu.VMEM((16, 16, B), f32),
    ]
    for rows, _ in RS_PARTS:
        for shapes in part_buffers(rows):
            scratch += [pltpu.VMEM(shape, f32) for shape in shapes]
    scratch += [
        pltpu.SemaphoreType.DMA((N_SEM,)),
        pltpu.SemaphoreType.DMA((N_SEM,)),
        pltpu.SemaphoreType.DMA((2, 16)),
        pltpu.SemaphoreType.DMA((6,)),
    ]
    return pl.pallas_call(
        functools.partial(kernel, scale),
        out_shape=(
            pltpu.VMEM((2048, n_rows), f32),
            pltpu.VMEM((16, 16 * B), f32),
        ),
        in_specs=[pl.BlockSpec(memory_space=pltpu.HBM)] * 2,
        out_specs=(
            pl.BlockSpec(memory_space=pltpu.VMEM),
            pl.BlockSpec(memory_space=pltpu.VMEM),
        ),
        scratch_shapes=scratch,
        compiler_params=pltpu.CompilerParams(
            collective_id=0, has_side_effects=True, vmem_limit_bytes=40 * 2**20
        ),
        cost_estimate=pl.CostEstimate(
            flops=2 * 2048 * n_rows * 2048 * 2, bytes_accessed=20 * 2**20, transcendentals=0
        ),
    )(*(pltpu.with_memory_space_constraint(a, pltpu.HBM) for a in (queries, training)))


def solution(mesh):
    in_specs = (P(("blk", "grp"), None), P(("blk", "grp"), None))
    out_specs = (P(None, ("blk", "grp")), P(("blk", "grp"), None))
    return jax.shard_map(
        functools.partial(local, 1.0 / 131072),
        mesh=mesh,
        in_specs=in_specs,
        out_specs=out_specs,
        check_vma=False,
    )
```

```python
import functools

import jax
import jax.numpy as jnp
from jax import lax
from jax.experimental import pallas as pl
from jax.experimental.pallas import tpu as pltpu
from jax.sharding import PartitionSpec as P

MESH = pl.DeviceIdType.MESH
ALL = pl.ds(0, 4)
AXES = ("z", "x", "y")
B = 128
CH = 136
AG_PARTS = (((0, 640), "yxz"), ((640, 1280), "zyx"), ((1280, 2048), "xzy"))
RS_PARTS = (((0, 48), "zxy"), ((48, 96), "xyz"), ((96, 136), "yzx"))
N_SEM = 192
HERE = 3
STAGES = (2, 1, 3, 0)
ORDER = (
    "gather",
    "share 0",
    "share 1",
    "gram 2",
    "share 2",
    "join 0",
    "gather",
    "join 1",
    "gram 3",
    "share 3",
    "pass 0",
    "join 2",
    "pass 1",
    "join 3",
    "pass 2",
    "pass 3",
    "gather",
    "reduce",
    "gather",
    "reduce",
    "gather",
    "gather",
    "reduce",
    "exchange",
    "scores 0",
    "scores 1",
    "scores 2",
)


def stored(axis, i):
    return lax.rem(i, 2) * 2 + lax.div(i, 2) if axis == "y" else i


class Net:
    def __init__(self, ssem, rsem):
        blk, grp = lax.axis_index("blk"), lax.axis_index("grp")
        self.at = {
            "z": lax.div(blk, 8),
            "x": lax.rem(lax.div(blk, 2), 4),
            "y": lax.div(grp, 2) * 2 + lax.rem(blk, 2),
        }
        self.core = lax.rem(grp, 2)
        self.group = lax.div(blk, 2)
        self.k = lax.rem(blk, 2) * 4 + grp
        self.ssem, self.rsem = ssem, rsem
        self.count = 0
        self.sent = []

    def device(self, core=None, **moved):
        at = {**self.at, **moved}
        core = self.core if core is None else core
        return (at["z"] * 8 + at["x"] * 2 + lax.rem(at["y"], 2), lax.div(at["y"], 2) * 2 + core)

    def hop(self, axis, by):
        return lax.rem(self.at[axis] + by + 4, 4)

    def neighbour(self, axis, by):
        return self.device(**{axis: self.hop(axis, by)})

    def sibling(self):
        return self.device(core=1 - self.core)

    def send(self, src, dst, to):
        t = self.count
        self.count += 1
        copy = pltpu.make_async_remote_copy(
            src_ref=src,
            dst_ref=dst,
            send_sem=self.ssem.at[t],
            recv_sem=self.rsem.at[t],
            device_id=to,
            device_id_type=MESH,
        )
        copy.start()
        self.sent.append(copy)
        return copy


def member(group, k):
    return (group * 2 + lax.div(k, 4), lax.rem(k, 4))


def gather_part(net, q, cols, order):
    lo, hi = cols

    def region(idx, c=None):
        at = [idx[a] for a in AXES]
        return q.at[at[0], at[1], at[2], net.core, :, pl.ds(lo, hi - lo)] if c is None else q.at[
            at[0], at[1], at[2], net.core, :, pl.ds(*c)
        ]

    def halves(idx):
        free = [a for a in AXES if isinstance(idx[a], pl.Slice)]
        if free:
            return [region({**idx, free[0]: pl.ds(2 * h, 2)}) for h in range(2)]
        mid = (hi - lo) // 256 * 128
        return [region(idx, (lo, mid)), region(idx, (lo + mid, hi - lo - mid))]

    idx = {a: stored(a, net.at[a]) for a in AXES}
    to_sibling = []

    def spread(axis):
        here = region(idx)
        return [net.send(here, here, net.neighbour(axis, by)) for by in (2, 1, -1)]

    def ahead(at):
        here = region(at)
        return [net.send(here, here, net.neighbour(order[2], by)) for by in (1, -1)]

    def hand(at):
        to_sibling.append(net.send(region(at), region(at), net.sibling()))

    first = spread(order[0])
    yield
    for copy in first:
        copy.wait_recv()
    idx = {**idx, order[0]: ALL}
    second = spread(order[1])
    third = [ahead(idx)]
    hand(idx)
    yield
    for copy in second:
        copy.wait_recv()
    for by in (1, -1, 2):
        at = {**idx, order[1]: stored(order[1], net.hop(order[1], by))}
        third.append(ahead(at))
        hand(at)
    yield
    idx = {**idx, order[1]: ALL}
    axis = order[2]
    low, high, far = ({**idx, axis: stored(axis, net.hop(axis, by))} for by in (-1, 1, 2))
    for up, _ in third:
        up.wait_recv()
    src = halves(low)[0]
    on_up = net.send(src, src, net.neighbour(axis, 1))
    for _, down in third:
        down.wait_recv()
    src = halves(high)[1]
    on_down = net.send(src, src, net.neighbour(axis, -1))
    hand(low)
    hand(high)
    yield
    on_up.wait_recv()
    on_down.wait_recv()
    hand(far)
    yield
    for copy in to_sibling:
        copy.wait_recv()


class Reduce:
    def __init__(self, net, p, bufs, rows, order):
        self.net, self.p, self.bufs, self.rows, self.order = net, p, bufs, rows, order
        self.up, self.down = net.neighbour(order[0], 1), net.neighbour(order[0], -1)
        self.copies = {}

    def region(self, idx):
        lo, hi = self.rows
        at = [idx[a] for a in AXES]
        return self.p.at[at[0], at[1], at[2], self.net.core, pl.ds(lo, hi - lo)]

    def halves(self, stage, by):
        first = self.order[0]
        if first == "z":
            idx = {"z": self.net.hop("z", by), "x": ALL, "y": ALL}
        else:
            idx = {"x": ALL, "y": ALL, "z": self.net.hop("z", STAGES[stage])}
            idx[first] = stored(first, self.net.hop(first, by))
        free = next(a for a in AXES if isinstance(idx[a], pl.Slice))
        return [self.region({**idx, free: pl.ds(2 * h, 2)}) for h in range(2)]

    def go(self, stage, name, src, slot, to):
        dst = self.bufs[0][slot]
        if self.order[0] != "z":
            dst = dst.at[stage]
        self.copies[stage, name] = self.net.send(src, dst, to), dst

    def start(self, stage):
        whole = self.order[0] != "z"
        if whole or STAGES[stage] == 2:
            far = self.halves(stage, 2)
            self.go(stage, "via_up", far[0], 0, self.up)
            self.go(stage, "via_down", far[1], 1, self.down)
        if whole or STAGES[stage] == 1:
            self.go(stage, "own_up", self.halves(stage, 1)[1], 2, self.up)
        if whole or STAGES[stage] == 3:
            self.go(stage, "own_down", self.halves(stage, -1)[0], 3, self.down)

    def add(self, stage, name, ref):
        copy, dst = self.copies[stage, name]
        copy.wait_recv()
        ref[...] += dst[...]

    def pass_on(self, stage):
        whole = self.order[0] != "z"
        via = stage if whole else STAGES.index(2)
        if whole or STAGES[stage] == 1:
            high = self.halves(stage, 1)[0]
            self.add(via, "via_up", high)
            self.go(stage, "sum_up", high, 4, self.up)
        if whole or STAGES[stage] == 3:
            low = self.halves(stage, -1)[1]
            self.add(via, "via_down", low)
            self.go(stage, "sum_down", low, 5, self.down)

    def rest(self):
        net, order = self.net, self.order
        whole = order[0] != "z"
        for stage in range(4) if whole else (None,):
            mine = self.halves(stage, 0)
            for name, h, at in (
                ("own_up", 1, STAGES.index(1)),
                ("sum_down", 1, STAGES.index(3)),
                ("own_down", 0, STAGES.index(3)),
                ("sum_up", 0, STAGES.index(1)),
            ):
                self.add(stage if whole else at, name, mine[h])
        idx = {**{a: ALL for a in AXES}, order[0]: stored(order[0], net.at[order[0]])}
        for axis, buf in zip(order[1:], self.bufs[1:], strict=True):
            copies = [
                net.send(
                    self.region({**idx, axis: stored(axis, net.hop(axis, by))}),
                    buf[i],
                    net.neighbour(axis, by),
                )
                for i, by in enumerate((2, 1, -1))
            ]
            idx = {**idx, axis: stored(axis, net.at[axis])}
            yield
            for copy in copies:
                copy.wait_recv()
            self.region(idx)[...] += buf[0][...] + buf[1][...] + buf[2][...]


def part_buffers(rows, order):
    n = rows[1] - rows[0]
    return [[(2, 4, n, B) if order[0] == "z" else (4, 2, n, B)] * 6, [(4, n, B)] * 3, [(n, B)] * 3]


def step_all(gens):
    left = False
    for g in list(gens):
        try:
            next(g)
            left = True
        except StopIteration:
            gens.remove(g)
    return left


def kernel(scale, *refs):
    (q_in, t_in, s, g_out, q, t, p, d2d, x, slots) = refs[:10]
    *flat, ssem, rsem, xsem, lsem = refs[10:]
    flat = iter(flat)
    bufs = [[[next(flat) for _ in shapes] for shapes in part_buffers(*part)] for part in RS_PARTS]
    net = Net(ssem, rsem)
    zi, xi, yi = (stored(a, net.at[a]) for a in AXES)
    core, group, k = net.core, net.group, net.k
    odd = lax.rem(group, 2)
    packed = jnp.logical_and(k == 0, odd != lax.div(group, 8))
    other = jnp.where(
        packed, group + 1 - 2 * odd, lax.rem(group + jnp.where(k == 0, 8, k), 16)
    )

    load_q = pltpu.make_async_copy(q_in, q.at[zi, xi, yi, core], lsem.at[0])
    load_q.start()
    load_t = pltpu.make_async_copy(t_in, t, lsem.at[1])
    load_t.start()

    barrier = pltpu.get_barrier_semaphore()

    def greet(device):
        pl.semaphore_signal(barrier, inc=1, device_id=device, device_id_type=MESH)

    for axis in AXES:
        greet(net.neighbour(axis, 1))
        greet(net.neighbour(axis, -1))
        greet(net.neighbour(axis, 2))
    greet(net.sibling())
    load_t.wait()

    p[:, :, :, :, pl.ds(B, 8)] = jnp.zeros((4, 4, 4, 2, 8, B), jnp.float32)
    row = lax.broadcasted_iota(jnp.int32, (B, B), 0)
    col = lax.broadcasted_iota(jnp.int32, (B, B), 1)

    def chunk(g, kk):
        return p.at[lax.div(g, 4), lax.rem(g, 4), kk // 2, kk % 2]

    def strip(i):
        left = t[:, pl.ds(pl.multiple_of(i * 256, 256), 256)]
        late = i >= 4
        g8 = 2 * i + jnp.where(late, 1, 0)
        gd = 2 * i + jnp.where(late, 0, 1)
        for j in range(5):
            jj = lax.rem(i + j, 8)
            right = t[:, pl.ds(pl.multiple_of(jj * 256, 256), 256)]
            prod = lax.dot_general(
                left, right, (((0,), (0,)), ((), ())), preferred_element_type=jnp.float32
            )
            blocks = {
                (r, c): prod[r * B : r * B + B, c * B : c * B + B] for r in range(2) for c in range(2)
            }
            for (r, c), block in blocks.items():
                if 1 <= 2 * j + c - r <= 7:
                    chunk(2 * i + r, 2 * j + c - r)[pl.ds(0, B), :] = block
            if j == 0:
                chunk(gd, 0)[pl.ds(0, B), :] = jnp.where(row <= col, blocks[0, 0], blocks[1, 1])
                chunk(gd, 0)[pl.ds(B, 1), :] = jnp.sum(
                    jnp.where(row == col, blocks[1, 1], 0.0), axis=0, keepdims=True
                )
            if j == 4:
                chunk(g8, 0)[pl.ds(0, B), :] = jnp.where(late, blocks[1, 1], blocks[0, 0])

    to_sibling = []

    def gram_rows(stage):
        z = net.hop("z", STAGES[stage])
        pl.loop(2 * z, 2 * z + 2)(strip)

    def share(stage):
        z = net.hop("z", STAGES[stage])
        to_sibling.append(net.send(p.at[z, :, :, 1 - core], d2d.at[stage], net.sibling()))

    def join(stage):
        z = net.hop("z", STAGES[stage])
        to_sibling[stage].wait_recv()

        @pl.loop(0, 4)
        def _(i):
            p[z, i, :, core] += d2d[stage, i]

        for part in parts:
            part.start(stage)

    def pass_on(stage):
        for part in parts:
            part.pass_on(stage)

    def scores(z):
        s[pl.ds(512 * z, 512), :] = lax.dot_general(
            q[z].reshape(512, 2048),
            t[...],
            (((1,), (1,)), ((), ())),
            preferred_element_type=jnp.float32,
        )

    last = []

    def exchange(_):
        mine = p[zi, xi, yi, core, pl.ds(0, B), :] * scale
        turned = mine.T
        diagonal = p[zi, xi, yi, core, pl.ds(B, 1), :] * scale
        first = jnp.where(row <= col, mine, turned)
        second = jnp.where(row > col, mine, jnp.where(row < col, turned, jnp.broadcast_to(diagonal, (B, B))))
        even = odd == 0
        x[0] = jnp.where(packed, jnp.where(even, first, second), mine).reshape(8, 16, B)
        x[1] = jnp.where(packed, jnp.where(even, second, first), turned).reshape(8, 16, B)
        own_slot = jnp.where(packed, group, other)
        other_slot = jnp.where(packed, other, group)
        slots[own_slot] = x[0, k]
        for m in range(1, 8):
            to = lax.rem(k + m, 8)
            copy = pltpu.make_async_remote_copy(
                src_ref=x.at[0, to],
                dst_ref=slots.at[own_slot],
                send_sem=xsem.at[0, m],
                recv_sem=xsem.at[1, m],
                device_id=member(group, to),
                device_id_type=MESH,
            )
            copy.start()
            last.append(copy)
        for m in range(8):
            copy = pltpu.make_async_remote_copy(
                src_ref=x.at[1, m],
                dst_ref=slots.at[other_slot],
                send_sem=xsem.at[0, 8 + m],
                recv_sem=xsem.at[1, 8 + k],
                device_id=member(other, jnp.int32(m)),
                device_id_type=MESH,
            )
            copy.start()
            last.append(copy)

    gather = [gather_part(net, q, *part) for part in AG_PARTS]
    parts = [Reduce(net, p, bufs[i], *part) for i, part in enumerate(RS_PARTS)]
    reduce = [part.rest() for part in parts]
    plan = {
        "gather": lambda _: step_all(gather),
        "reduce": lambda _: step_all(reduce),
        "gram": gram_rows,
        "share": share,
        "join": join,
        "pass": pass_on,
        "scores": scores,
        "exchange": exchange,
    }

    gram_rows(0)
    gram_rows(1)
    pl.semaphore_wait(barrier, 10)
    load_q.wait()
    for step in ORDER:
        name, *at = step.split()
        plan[name](int(at[0]) if at else None)
    assert not step_all(gather) and not step_all(reduce)

    for m in range(1, 16):
        pltpu.make_async_remote_copy(
            src_ref=x.at[0, 0],
            dst_ref=slots.at[0],
            send_sem=xsem.at[0, m],
            recv_sem=xsem.at[1, m],
            device_id=net.sibling(),
            device_id_type=MESH,
        ).wait_recv()
    for c in range(16):
        g_out[:, pl.ds(c * B, B)] = slots[c]
    for copy in last + net.sent:
        copy.wait_send()


def finish(s_in, g_in, q_in, t_in, s_out, g_out, last, sem):
    done = s_in.shape[0]
    moves = [
        pltpu.make_async_copy(s_in, s_out.at[pl.ds(0, done)], sem.at[0]),
        pltpu.make_async_copy(g_in, g_out, sem.at[1]),
    ]
    for move in moves:
        move.start()
    rows = 256
    for h in range(last.shape[0] // rows):
        here = pl.ds(h * rows, rows)
        last[here, :] = lax.dot_general(
            q_in[HERE + h // 2, pl.ds(h % 2 * 2, 2)].reshape(rows, q_in.shape[-1]),
            t_in[...],
            (((1,), (1,)), ((), ())),
            preferred_element_type=jnp.float32,
        )
        move = pltpu.make_async_copy(
            last.at[here], s_out.at[pl.ds(done + h * rows, rows)], sem.at[2 + h]
        )
        move.start()
        moves.append(move)
    for move in moves:
        move.wait()


def local(scale, queries, training):
    n_rows, width = training.shape
    f32, bf16 = jnp.float32, jnp.bfloat16
    vmem, hbm = pl.BlockSpec(memory_space=pltpu.VMEM), pl.BlockSpec(memory_space=pltpu.HBM)
    scratch = [
        pltpu.VMEM((4, 4, 4, 2, CH, B), f32),
        pltpu.VMEM((4, 4, 4, CH, B), f32),
        pltpu.VMEM((2, 8, 16, B), f32),
        pltpu.VMEM((16, 16, B), f32),
    ]
    for part in RS_PARTS:
        for shapes in part_buffers(*part):
            scratch += [pltpu.VMEM(shape, f32) for shape in shapes]
    scratch += [
        pltpu.SemaphoreType.DMA((N_SEM,)),
        pltpu.SemaphoreType.DMA((N_SEM,)),
        pltpu.SemaphoreType.DMA((2, 16)),
        pltpu.SemaphoreType.DMA((6,)),
    ]
    some, gram, q, t = pl.pallas_call(
        functools.partial(kernel, scale),
        out_shape=(
            pltpu.VMEM((512 * HERE, n_rows), f32),
            pltpu.VMEM((16, 16 * B), f32),
            pltpu.VMEM((4, 4, 4, 2, 16, width), bf16),
            pltpu.VMEM((n_rows, width), bf16),
        ),
        in_specs=[hbm] * 2,
        out_specs=(vmem,) * 4,
        scratch_shapes=scratch,
        compiler_params=pltpu.CompilerParams(
            collective_id=0, has_side_effects=True, vmem_limit_bytes=24 * 2**20
        ),
        cost_estimate=pl.CostEstimate(
            flops=2 * 2048 * n_rows * 2048 * 2, bytes_accessed=20 * 2**20, transcendentals=0
        ),
    )(*(pltpu.with_memory_space_constraint(a, pltpu.HBM) for a in (queries, training)))
    return pl.pallas_call(
        finish,
        out_shape=(
            jax.ShapeDtypeStruct((2048, n_rows), f32),
            jax.ShapeDtypeStruct((16, 16 * B), f32),
        ),
        in_specs=[vmem] * 4,
        out_specs=(hbm, hbm),
        scratch_shapes=[pltpu.VMEM((512 * (4 - HERE), n_rows), f32), pltpu.SemaphoreType.DMA((10,))],
        compiler_params=pltpu.CompilerParams(vmem_limit_bytes=16 * 2**20),
    )(some, gram, q, t)


def solution(mesh):
    in_specs = (P(("blk", "grp"), None), P(("blk", "grp"), None))
    out_specs = (P(None, ("blk", "grp")), P(("blk", "grp"), None))
    return jax.shard_map(
        functools.partial(local, 1.0 / 131072),
        mesh=mesh,
        in_specs=in_specs,
        out_specs=out_specs,
        check_vma=False,
    )
```

```python
import functools

import jax
import jax.numpy as jnp
from jax import lax
from jax.experimental import pallas as pl
from jax.experimental.pallas import tpu as pltpu
from jax.sharding import PartitionSpec as P

MESH = pl.DeviceIdType.MESH
ALL = pl.ds(0, 4)
AXES = ("z", "x", "y")
B = 128
CH = 136
AG_PARTS = (((0, 640), "yxz"), ((640, 1280), "zyx"), ((1280, 2048), "xzy"))
RS_PARTS = (((0, 48), "zxy"), ((48, 96), "xyz"), ((96, 136), "yzx"))
N_SEM = 192
HERE = 3
STAGES = (2, 1, 3, 0)
ORDER = (
    "gather",
    "share 0",
    "share 1",
    "gram 2",
    "share 2",
    "join 0",
    "gather",
    "join 1",
    "gram 3",
    "share 3",
    "pass 0",
    "join 2",
    "gather",
    "pass 1",
    "join 3",
    "pass 2",
    "pass 3",
    "gather",
    "reduce",
    "gather",
    "reduce",
    "drain 30",
    "gather",
    "reduce",
    "exchange",
    "gather",
    "scores 0",
    "scores 1",
    "scores 2",
)


def stored(axis, i):
    return lax.rem(i, 2) * 2 + lax.div(i, 2) if axis == "y" else i


class Net:
    def __init__(self, ssem, rsem):
        blk, grp = lax.axis_index("blk"), lax.axis_index("grp")
        self.at = {
            "z": lax.div(blk, 8),
            "x": lax.rem(lax.div(blk, 2), 4),
            "y": lax.div(grp, 2) * 2 + lax.rem(blk, 2),
        }
        self.core = lax.rem(grp, 2)
        self.group = lax.div(blk, 2)
        self.k = lax.rem(blk, 2) * 4 + grp
        self.ssem, self.rsem = ssem, rsem
        self.count = 0
        self.sent = []

    def device(self, core=None, **moved):
        at = {**self.at, **moved}
        core = self.core if core is None else core
        return (at["z"] * 8 + at["x"] * 2 + lax.rem(at["y"], 2), lax.div(at["y"], 2) * 2 + core)

    def hop(self, axis, by):
        return lax.rem(self.at[axis] + by + 4, 4)

    def neighbour(self, axis, by):
        return self.device(**{axis: self.hop(axis, by)})

    def sibling(self):
        return self.device(core=1 - self.core)

    def send(self, src, dst, to):
        t = self.count
        self.count += 1
        copy = pltpu.make_async_remote_copy(
            src_ref=src,
            dst_ref=dst,
            send_sem=self.ssem.at[t],
            recv_sem=self.rsem.at[t],
            device_id=to,
            device_id_type=MESH,
        )
        copy.start()
        self.sent.append(copy)
        return copy


def member(group, k):
    return (group * 2 + lax.div(k, 4), lax.rem(k, 4))


def gather_part(net, q, cols, order):
    lo, hi = cols

    def region(idx, c=None):
        at = [idx[a] for a in AXES]
        return q.at[at[0], at[1], at[2], net.core, :, pl.ds(lo, hi - lo)] if c is None else q.at[
            at[0], at[1], at[2], net.core, :, pl.ds(*c)
        ]

    def halves(idx):
        free = [a for a in AXES if isinstance(idx[a], pl.Slice)]
        if free:
            return [region({**idx, free[0]: pl.ds(2 * h, 2)}) for h in range(2)]
        mid = (hi - lo) // 256 * 128
        return [region(idx, (lo, mid)), region(idx, (lo + mid, hi - lo - mid))]

    idx = {a: stored(a, net.at[a]) for a in AXES}
    to_sibling = []

    def spread(axis):
        here = region(idx)
        return [net.send(here, here, net.neighbour(axis, by)) for by in (2, 1, -1)]

    def ahead(at):
        here = region(at)
        return [net.send(here, here, net.neighbour(order[2], by)) for by in (1, -1)]

    def hand(at):
        to_sibling.append(net.send(region(at), region(at), net.sibling()))

    first = spread(order[0])
    yield
    for copy in first:
        copy.wait_recv()
    idx = {**idx, order[0]: ALL}
    axis = order[1]
    here = region(idx)
    up, down = (net.send(here, here, net.neighbour(axis, by)) for by in (1, -1))
    third = [ahead(idx)]
    hand(idx)
    yield
    up.wait_recv()
    src = halves({**idx, axis: stored(axis, net.hop(axis, -1))})[0]
    on_up = net.send(src, src, net.neighbour(axis, 1))
    down.wait_recv()
    src = halves({**idx, axis: stored(axis, net.hop(axis, 1))})[1]
    on_down = net.send(src, src, net.neighbour(axis, -1))
    yield
    on_up.wait_recv()
    on_down.wait_recv()
    for by in (1, -1, 2):
        at = {**idx, order[1]: stored(order[1], net.hop(order[1], by))}
        third.append(ahead(at))
        hand(at)
    yield
    idx = {**idx, order[1]: ALL}
    axis = order[2]
    low, high, far = ({**idx, axis: stored(axis, net.hop(axis, by))} for by in (-1, 1, 2))
    for up, _ in third:
        up.wait_recv()
    src = halves(low)[0]
    on_up = net.send(src, src, net.neighbour(axis, 1))
    for _, down in third:
        down.wait_recv()
    src = halves(high)[1]
    on_down = net.send(src, src, net.neighbour(axis, -1))
    hand(low)
    hand(high)
    yield
    on_up.wait_recv()
    on_down.wait_recv()
    hand(far)
    yield
    for copy in to_sibling:
        copy.wait_recv()


class Reduce:
    def __init__(self, net, p, bufs, rows, order):
        self.net, self.p, self.bufs, self.rows, self.order = net, p, bufs, rows, order
        self.up, self.down = net.neighbour(order[0], 1), net.neighbour(order[0], -1)
        self.copies = {}

    def region(self, idx):
        lo, hi = self.rows
        at = [idx[a] for a in AXES]
        return self.p.at[at[0], at[1], at[2], self.net.core, pl.ds(lo, hi - lo)]

    def halves(self, stage, by):
        first = self.order[0]
        if first == "z":
            idx = {"z": self.net.hop("z", by), "x": ALL, "y": ALL}
        else:
            idx = {"x": ALL, "y": ALL, "z": self.net.hop("z", STAGES[stage])}
            idx[first] = stored(first, self.net.hop(first, by))
        free = next(a for a in AXES if isinstance(idx[a], pl.Slice))
        return [self.region({**idx, free: pl.ds(2 * h, 2)}) for h in range(2)]

    def go(self, stage, name, src, slot, to):
        dst = self.bufs[0][slot]
        if self.order[0] != "z":
            dst = dst.at[stage]
        self.copies[stage, name] = self.net.send(src, dst, to), dst

    def start(self, stage):
        whole = self.order[0] != "z"
        if whole or STAGES[stage] == 2:
            far = self.halves(stage, 2)
            self.go(stage, "via_up", far[0], 0, self.up)
            self.go(stage, "via_down", far[1], 1, self.down)
        if whole or STAGES[stage] == 1:
            self.go(stage, "own_up", self.halves(stage, 1)[1], 2, self.up)
        if whole or STAGES[stage] == 3:
            self.go(stage, "own_down", self.halves(stage, -1)[0], 3, self.down)

    def add(self, ref, *arrived):
        for at in arrived:
            self.copies[at][0].wait_recv()
        total = ref[...]
        for at in arrived:
            total = total + self.copies[at][1][...]
        ref[...] = total

    def pass_on(self, stage):
        whole = self.order[0] != "z"
        via = stage if whole else STAGES.index(2)
        if whole or STAGES[stage] == 1:
            high = self.halves(stage, 1)[0]
            self.add(high, (via, "via_up"))
            self.go(stage, "sum_up", high, 4, self.up)
        if whole or STAGES[stage] == 3:
            low = self.halves(stage, -1)[1]
            self.add(low, (via, "via_down"))
            self.go(stage, "sum_down", low, 5, self.down)

    def rest(self):
        net, order = self.net, self.order
        whole = order[0] != "z"
        for stage in range(4) if whole else (None,):
            mine = self.halves(stage, 0)
            one, three = (stage, stage) if whole else (STAGES.index(1), STAGES.index(3))
            self.add(mine[1], (one, "own_up"), (three, "sum_down"))
            self.add(mine[0], (three, "own_down"), (one, "sum_up"))
        idx = {**{a: ALL for a in AXES}, order[0]: stored(order[0], net.at[order[0]])}
        for axis, buf in zip(order[1:], self.bufs[1:], strict=True):
            copies = [
                net.send(
                    self.region({**idx, axis: stored(axis, net.hop(axis, by))}),
                    buf[i],
                    net.neighbour(axis, by),
                )
                for i, by in enumerate((2, 1, -1))
            ]
            idx = {**idx, axis: stored(axis, net.at[axis])}
            yield
            for copy in copies:
                copy.wait_recv()
            self.region(idx)[...] += buf[0][...] + buf[1][...] + buf[2][...]


def part_buffers(rows, order):
    n = rows[1] - rows[0]
    return [[(2, 4, n, B) if order[0] == "z" else (4, 2, n, B)] * 6, [(4, n, B)] * 3, [(n, B)] * 3]


def step_all(gens):
    left = False
    for g in list(gens):
        try:
            next(g)
            left = True
        except StopIteration:
            gens.remove(g)
    return left


def kernel(scale, *refs):
    (q_in, t_in, s, g_out, q, t, p, d2d, x, slots) = refs[:10]
    *flat, ssem, rsem, xsem, lsem = refs[10:]
    flat = iter(flat)
    bufs = [[[next(flat) for _ in shapes] for shapes in part_buffers(*part)] for part in RS_PARTS]
    net = Net(ssem, rsem)
    zi, xi, yi = (stored(a, net.at[a]) for a in AXES)
    core, group, k = net.core, net.group, net.k
    odd = lax.rem(group, 2)
    packed = jnp.logical_and(k == 0, odd != lax.div(group, 8))
    other = jnp.where(
        packed, group + 1 - 2 * odd, lax.rem(group + jnp.where(k == 0, 8, k), 16)
    )

    load_q = pltpu.make_async_copy(q_in, q.at[zi, xi, yi, core], lsem.at[0])
    load_q.start()
    load_t = pltpu.make_async_copy(t_in, t, lsem.at[1])
    load_t.start()

    barrier = pltpu.get_barrier_semaphore()

    def greet(device):
        pl.semaphore_signal(barrier, inc=1, device_id=device, device_id_type=MESH)

    for axis in AXES:
        greet(net.neighbour(axis, 2))
    for axis in AXES:
        greet(net.neighbour(axis, 1))
        greet(net.neighbour(axis, -1))
    greet(net.sibling())
    load_t.wait()

    p[:, :, :, :, pl.ds(B, 8)] = jnp.zeros((4, 4, 4, 2, 8, B), jnp.float32)
    row = lax.broadcasted_iota(jnp.int32, (B, B), 0)
    col = lax.broadcasted_iota(jnp.int32, (B, B), 1)

    def chunk(g, kk):
        return p.at[lax.div(g, 4), lax.rem(g, 4), kk // 2, kk % 2]

    def strip(i):
        left = t[:, pl.ds(pl.multiple_of(i * 256, 256), 256)]
        late = i >= 4
        g8 = 2 * i + jnp.where(late, 1, 0)
        gd = 2 * i + jnp.where(late, 0, 1)
        for j in range(5):
            jj = lax.rem(i + j, 8)
            right = t[:, pl.ds(pl.multiple_of(jj * 256, 256), 256)]
            prod = lax.dot_general(
                left, right, (((0,), (0,)), ((), ())), preferred_element_type=jnp.float32
            )
            blocks = {
                (r, c): prod[r * B : r * B + B, c * B : c * B + B] for r in range(2) for c in range(2)
            }
            for (r, c), block in blocks.items():
                if 1 <= 2 * j + c - r <= 7:
                    chunk(2 * i + r, 2 * j + c - r)[pl.ds(0, B), :] = block
            if j == 0:
                chunk(gd, 0)[pl.ds(0, B), :] = jnp.where(row <= col, blocks[0, 0], blocks[1, 1])
                chunk(gd, 0)[pl.ds(B, 1), :] = jnp.sum(
                    jnp.where(row == col, blocks[1, 1], 0.0), axis=0, keepdims=True
                )
            if j == 4:
                chunk(g8, 0)[pl.ds(0, B), :] = jnp.where(late, blocks[1, 1], blocks[0, 0])

    to_sibling = []

    def gram_rows(stage):
        z = net.hop("z", STAGES[stage])
        pl.loop(2 * z, 2 * z + 2)(strip)

    def share(stage):
        z = net.hop("z", STAGES[stage])
        to_sibling.append(net.send(p.at[z, :, :, 1 - core], d2d.at[stage], net.sibling()))

    def join(stage):
        z = net.hop("z", STAGES[stage])
        to_sibling[stage].wait_recv()

        @pl.loop(0, 4)
        def _(i):
            p[z, i, :, core] += d2d[stage, i]

        for part in parts:
            part.start(stage)

    def pass_on(stage):
        for part in parts:
            part.pass_on(stage)

    def scores(z):
        s[pl.ds(512 * z, 512), :] = lax.dot_general(
            q[z].reshape(512, 2048),
            t[...],
            (((1,), (1,)), ((), ())),
            preferred_element_type=jnp.float32,
        )

    last = []

    def exchange(_):
        mine = p[zi, xi, yi, core, pl.ds(0, B), :] * scale
        turned = mine.T
        diagonal = p[zi, xi, yi, core, pl.ds(B, 1), :] * scale
        first = jnp.where(row <= col, mine, turned)
        second = jnp.where(row > col, mine, jnp.where(row < col, turned, jnp.broadcast_to(diagonal, (B, B))))
        even = odd == 0
        x[0] = jnp.where(packed, jnp.where(even, first, second), mine).reshape(8, 16, B)
        x[1] = jnp.where(packed, jnp.where(even, second, first), turned).reshape(8, 16, B)
        own_slot = jnp.where(packed, group, other)
        other_slot = jnp.where(packed, other, group)
        slots[own_slot] = x[0, k]
        for m in range(8):
            copy = pltpu.make_async_remote_copy(
                src_ref=x.at[1, m],
                dst_ref=slots.at[other_slot],
                send_sem=xsem.at[0, 8 + m],
                recv_sem=xsem.at[1, 8 + k],
                device_id=member(other, jnp.int32(m)),
                device_id_type=MESH,
            )
            copy.start()
            last.append(copy)
        for m in range(1, 8):
            to = lax.rem(k + m, 8)
            copy = pltpu.make_async_remote_copy(
                src_ref=x.at[0, to],
                dst_ref=slots.at[own_slot],
                send_sem=xsem.at[0, m],
                recv_sem=xsem.at[1, m],
                device_id=member(group, to),
                device_id_type=MESH,
            )
            copy.start()
            last.append(copy)

    gather = [gather_part(net, q, *part) for part in AG_PARTS]
    parts = [Reduce(net, p, bufs[i], *part) for i, part in enumerate(RS_PARTS)]
    reduce = [part.rest() for part in parts]
    def drain(kept):
        for copy in net.sent[:-kept]:
            copy.wait_send()
        del net.sent[:-kept]

    plan = {
        "drain": drain,
        "gather": lambda _: step_all(gather),
        "reduce": lambda _: step_all(reduce),
        "gram": gram_rows,
        "share": share,
        "join": join,
        "pass": pass_on,
        "scores": scores,
        "exchange": exchange,
    }

    gram_rows(0)
    gram_rows(1)
    pl.semaphore_wait(barrier, 10)
    load_q.wait()
    for step in ORDER:
        name, *at = step.split()
        plan[name](int(at[0]) if at else None)
    assert not step_all(gather) and not step_all(reduce)

    for m in range(1, 16):
        pltpu.make_async_remote_copy(
            src_ref=x.at[0, 0],
            dst_ref=slots.at[0],
            send_sem=xsem.at[0, m],
            recv_sem=xsem.at[1, m],
            device_id=net.sibling(),
            device_id_type=MESH,
        ).wait_recv()
    for c in range(16):
        g_out[:, pl.ds(c * B, B)] = slots[c]
    for copy in last + net.sent:
        copy.wait_send()


def finish(s_in, g_in, q_in, t_in, s_out, g_out, last, sem):
    done = s_in.shape[0]
    moves = [
        pltpu.make_async_copy(s_in, s_out.at[pl.ds(0, done)], sem.at[0]),
        pltpu.make_async_copy(g_in, g_out, sem.at[1]),
    ]
    for move in moves:
        move.start()
    rows = 256
    for h in range(last.shape[0] // rows):
        here = pl.ds(h * rows, rows)
        last[here, :] = lax.dot_general(
            q_in[HERE + h // 2, pl.ds(h % 2 * 2, 2)].reshape(rows, q_in.shape[-1]),
            t_in[...],
            (((1,), (1,)), ((), ())),
            preferred_element_type=jnp.float32,
        )
        move = pltpu.make_async_copy(
            last.at[here], s_out.at[pl.ds(done + h * rows, rows)], sem.at[2 + h]
        )
        move.start()
        moves.append(move)
    for move in moves:
        move.wait()


def local(scale, queries, training):
    n_rows, width = training.shape
    f32, bf16 = jnp.float32, jnp.bfloat16
    vmem, hbm = pl.BlockSpec(memory_space=pltpu.VMEM), pl.BlockSpec(memory_space=pltpu.HBM)
    scratch = [
        pltpu.VMEM((4, 4, 4, 2, CH, B), f32),
        pltpu.VMEM((4, 4, 4, CH, B), f32),
        pltpu.VMEM((2, 8, 16, B), f32),
        pltpu.VMEM((16, 16, B), f32),
    ]
    for part in RS_PARTS:
        for shapes in part_buffers(*part):
            scratch += [pltpu.VMEM(shape, f32) for shape in shapes]
    scratch += [
        pltpu.SemaphoreType.DMA((N_SEM,)),
        pltpu.SemaphoreType.DMA((N_SEM,)),
        pltpu.SemaphoreType.DMA((2, 16)),
        pltpu.SemaphoreType.DMA((6,)),
    ]
    some, gram, q, t = pl.pallas_call(
        functools.partial(kernel, scale),
        out_shape=(
            pltpu.VMEM((512 * HERE, n_rows), f32),
            pltpu.VMEM((16, 16 * B), f32),
            pltpu.VMEM((4, 4, 4, 2, 16, width), bf16),
            pltpu.VMEM((n_rows, width), bf16),
        ),
        in_specs=[hbm] * 2,
        out_specs=(vmem,) * 4,
        scratch_shapes=scratch,
        compiler_params=pltpu.CompilerParams(
            collective_id=0, has_side_effects=True, vmem_limit_bytes=24 * 2**20
        ),
        cost_estimate=pl.CostEstimate(
            flops=2 * 2048 * n_rows * 2048 * 2, bytes_accessed=20 * 2**20, transcendentals=0
        ),
    )(*(pltpu.with_memory_space_constraint(a, pltpu.HBM) for a in (queries, training)))
    return pl.pallas_call(
        finish,
        out_shape=(
            jax.ShapeDtypeStruct((2048, n_rows), f32),
            jax.ShapeDtypeStruct((16, 16 * B), f32),
        ),
        in_specs=[vmem] * 4,
        out_specs=(hbm, hbm),
        scratch_shapes=[pltpu.VMEM((512 * (4 - HERE), n_rows), f32), pltpu.SemaphoreType.DMA((10,))],
        compiler_params=pltpu.CompilerParams(vmem_limit_bytes=16 * 2**20),
    )(some, gram, q, t)


def solution(mesh):
    in_specs = (P(("blk", "grp"), None), P(("blk", "grp"), None))
    out_specs = (P(None, ("blk", "grp")), P(("blk", "grp"), None))
    return jax.shard_map(
        functools.partial(local, 1.0 / 131072),
        mesh=mesh,
        in_specs=in_specs,
        out_specs=out_specs,
        check_vma=False,
    )
```

```python
import functools

import jax
import jax.numpy as jnp
from jax import lax
from jax.experimental import pallas as pl
from jax.experimental.pallas import tpu as pltpu
from jax.sharding import PartitionSpec as P

MESH = pl.DeviceIdType.MESH
ALL = pl.ds(0, 4)
AXES = ("z", "x", "y")
B = 128
CH = 136
AG_PARTS = (((0, 640), "yxz"), ((640, 1280), "zyx"), ((1280, 2048), "xzy"))
RS_PARTS = (((0, 48), "zxy"), ((48, 96), "xyz"), ((96, 136), "yzx"))
N_SEM = 192
HERE = 3
STAGES = (2, 1, 3, 0)
ORDER = (
    "gather",
    "share 0",
    "share 1",
    "gram 2",
    "share 2",
    "join 0",
    "gather",
    "join 1",
    "gram 3",
    "share 3",
    "pass 0",
    "join 2",
    "gather",
    "pass 1",
    "join 3",
    "pass 2",
    "pass 3",
    "reduce",
    "gather",
    "reduce",
    "drain 30",
    "gather",
    "reduce",
    "exchange",
    "gather",
    "scores 0",
    "scores 1",
    "scores 2",
)


def stored(axis, i):
    return lax.rem(i, 2) * 2 + lax.div(i, 2) if axis == "y" else i


class Net:
    def __init__(self, ssem, rsem):
        blk, grp = lax.axis_index("blk"), lax.axis_index("grp")
        self.at = {
            "z": lax.div(blk, 8),
            "x": lax.rem(lax.div(blk, 2), 4),
            "y": lax.div(grp, 2) * 2 + lax.rem(blk, 2),
        }
        self.core = lax.rem(grp, 2)
        self.group = lax.div(blk, 2)
        self.k = lax.rem(blk, 2) * 4 + grp
        self.ssem, self.rsem = ssem, rsem
        self.count = 0
        self.sent = []

    def device(self, core=None, **moved):
        at = {**self.at, **moved}
        core = self.core if core is None else core
        return (at["z"] * 8 + at["x"] * 2 + lax.rem(at["y"], 2), lax.div(at["y"], 2) * 2 + core)

    def hop(self, axis, by):
        return lax.rem(self.at[axis] + by + 4, 4)

    def neighbour(self, axis, by):
        return self.device(**{axis: self.hop(axis, by)})

    def sibling(self):
        return self.device(core=1 - self.core)

    def send(self, src, dst, to):
        t = self.count
        self.count += 1
        copy = pltpu.make_async_remote_copy(
            src_ref=src,
            dst_ref=dst,
            send_sem=self.ssem.at[t],
            recv_sem=self.rsem.at[t],
            device_id=to,
            device_id_type=MESH,
        )
        copy.start()
        self.sent.append(copy)
        return copy


def member(group, k):
    return (group * 2 + lax.div(k, 4), lax.rem(k, 4))


def gather_part(net, q, cols, order):
    lo, hi = cols

    def region(idx, c=None):
        at = [idx[a] for a in AXES]
        return q.at[at[0], at[1], at[2], net.core, :, pl.ds(lo, hi - lo)] if c is None else q.at[
            at[0], at[1], at[2], net.core, :, pl.ds(*c)
        ]

    def halves(idx):
        free = [a for a in AXES if isinstance(idx[a], pl.Slice)]
        if free:
            return [region({**idx, free[0]: pl.ds(2 * h, 2)}) for h in range(2)]
        mid = (hi - lo) // 256 * 128
        return [region(idx, (lo, mid)), region(idx, (lo + mid, hi - lo - mid))]

    idx = {a: stored(a, net.at[a]) for a in AXES}
    to_sibling = []

    def spread(axis):
        here = region(idx)
        return [net.send(here, here, net.neighbour(axis, by)) for by in (2, 1, -1)]

    def ahead(at):
        here = region(at)
        return [net.send(here, here, net.neighbour(order[2], by)) for by in (1, -1)]

    def hand(at):
        to_sibling.append(net.send(region(at), region(at), net.sibling()))

    first = spread(order[0])
    yield
    for copy in first:
        copy.wait_recv()
    idx = {**idx, order[0]: ALL}
    axis = order[1]
    here = region(idx)
    up, down = (net.send(here, here, net.neighbour(axis, by)) for by in (1, -1))
    third = [ahead(idx)]
    hand(idx)
    yield
    up.wait_recv()
    src = halves({**idx, axis: stored(axis, net.hop(axis, -1))})[0]
    on_up = net.send(src, src, net.neighbour(axis, 1))
    down.wait_recv()
    src = halves({**idx, axis: stored(axis, net.hop(axis, 1))})[1]
    on_down = net.send(src, src, net.neighbour(axis, -1))
    yield
    on_up.wait_recv()
    on_down.wait_recv()
    for by in (1, -1, 2):
        at = {**idx, order[1]: stored(order[1], net.hop(order[1], by))}
        third.append(ahead(at))
        hand(at)
    yield
    idx = {**idx, order[1]: ALL}
    axis = order[2]
    low, high, far = ({**idx, axis: stored(axis, net.hop(axis, by))} for by in (-1, 1, 2))
    for up, _ in third:
        up.wait_recv()
    src = halves(low)[0]
    on_up = net.send(src, src, net.neighbour(axis, 1))
    for _, down in third:
        down.wait_recv()
    src = halves(high)[1]
    on_down = net.send(src, src, net.neighbour(axis, -1))
    hand(low)
    hand(high)
    yield
    on_up.wait_recv()
    on_down.wait_recv()
    hand(far)
    yield
    for copy in to_sibling:
        copy.wait_recv()


class Reduce:
    def __init__(self, net, p, bufs, rows, order):
        self.net, self.p, self.bufs, self.rows, self.order = net, p, bufs, rows, order
        self.up, self.down = net.neighbour(order[0], 1), net.neighbour(order[0], -1)
        self.copies = {}

    def region(self, idx):
        lo, hi = self.rows
        at = [idx[a] for a in AXES]
        return self.p.at[at[0], at[1], at[2], self.net.core, pl.ds(lo, hi - lo)]

    def halves(self, stage, by):
        first = self.order[0]
        if first == "z":
            idx = {"z": self.net.hop("z", by), "x": ALL, "y": ALL}
        else:
            idx = {"x": ALL, "y": ALL, "z": self.net.hop("z", STAGES[stage])}
            idx[first] = stored(first, self.net.hop(first, by))
        free = next(a for a in AXES if isinstance(idx[a], pl.Slice))
        return [self.region({**idx, free: pl.ds(2 * h, 2)}) for h in range(2)]

    def go(self, stage, name, src, slot, to):
        dst = self.bufs[0][slot]
        if self.order[0] != "z":
            dst = dst.at[stage]
        self.copies[stage, name] = self.net.send(src, dst, to), dst

    def start(self, stage):
        whole = self.order[0] != "z"
        if whole or STAGES[stage] == 2:
            far = self.halves(stage, 2)
            self.go(stage, "via_up", far[0], 0, self.up)
            self.go(stage, "via_down", far[1], 1, self.down)
        if whole or STAGES[stage] == 1:
            self.go(stage, "own_up", self.halves(stage, 1)[1], 2, self.up)
        if whole or STAGES[stage] == 3:
            self.go(stage, "own_down", self.halves(stage, -1)[0], 3, self.down)

    def add(self, ref, *arrived):
        for at in arrived:
            self.copies[at][0].wait_recv()
        total = ref[...]
        for at in arrived:
            total = total + self.copies[at][1][...]
        ref[...] = total

    def pass_on(self, stage):
        whole = self.order[0] != "z"
        via = stage if whole else STAGES.index(2)
        if whole or STAGES[stage] == 1:
            high = self.halves(stage, 1)[0]
            self.add(high, (via, "via_up"))
            self.go(stage, "sum_up", high, 4, self.up)
        if whole or STAGES[stage] == 3:
            low = self.halves(stage, -1)[1]
            self.add(low, (via, "via_down"))
            self.go(stage, "sum_down", low, 5, self.down)

    def rest(self):
        net, order = self.net, self.order
        whole = order[0] != "z"
        for stage in range(4) if whole else (None,):
            mine = self.halves(stage, 0)
            one, three = (stage, stage) if whole else (STAGES.index(1), STAGES.index(3))
            self.add(mine[1], (one, "own_up"), (three, "sum_down"))
            self.add(mine[0], (three, "own_down"), (one, "sum_up"))
        idx = {**{a: ALL for a in AXES}, order[0]: stored(order[0], net.at[order[0]])}
        for axis, buf in zip(order[1:], self.bufs[1:], strict=True):
            copies = [
                net.send(
                    self.region({**idx, axis: stored(axis, net.hop(axis, by))}),
                    buf[i],
                    net.neighbour(axis, by),
                )
                for i, by in enumerate((2, 1, -1))
            ]
            idx = {**idx, axis: stored(axis, net.at[axis])}
            yield
            for copy in copies:
                copy.wait_recv()
            self.region(idx)[...] += buf[0][...] + buf[1][...] + buf[2][...]


def part_buffers(rows, order):
    n = rows[1] - rows[0]
    return [[(2, 4, n, B) if order[0] == "z" else (4, 2, n, B)] * 6, [(4, n, B)] * 3, [(n, B)] * 3]


def step_all(gens):
    left = False
    for g in list(gens):
        try:
            next(g)
            left = True
        except StopIteration:
            gens.remove(g)
    return left


def kernel(scale, *refs):
    (q_in, t_in, s, g_out, q, t, p, d2d, x, slots) = refs[:10]
    *flat, ssem, rsem, xsem, lsem = refs[10:]
    flat = iter(flat)
    bufs = [[[next(flat) for _ in shapes] for shapes in part_buffers(*part)] for part in RS_PARTS]
    net = Net(ssem, rsem)
    zi, xi, yi = (stored(a, net.at[a]) for a in AXES)
    core, group, k = net.core, net.group, net.k
    odd = lax.rem(group, 2)
    packed = jnp.logical_and(k == 0, odd != lax.div(group, 8))
    other = jnp.where(
        packed, group + 1 - 2 * odd, lax.rem(group + jnp.where(k == 0, 8, k), 16)
    )

    load_q = pltpu.make_async_copy(q_in, q.at[zi, xi, yi, core], lsem.at[0])
    load_q.start()
    load_t = pltpu.make_async_copy(t_in, t, lsem.at[1])
    load_t.start()

    barrier = pltpu.get_barrier_semaphore()

    def greet(device):
        pl.semaphore_signal(barrier, inc=1, device_id=device, device_id_type=MESH)

    for axis in AXES:
        greet(net.neighbour(axis, 2))
    for axis in AXES:
        greet(net.neighbour(axis, 1))
        greet(net.neighbour(axis, -1))
    greet(net.sibling())
    load_t.wait()

    p[:, :, :, :, pl.ds(B, 8)] = jnp.zeros((4, 4, 4, 2, 8, B), jnp.float32)
    row = lax.broadcasted_iota(jnp.int32, (B, B), 0)
    col = lax.broadcasted_iota(jnp.int32, (B, B), 1)

    def chunk(g, kk):
        return p.at[lax.div(g, 4), lax.rem(g, 4), kk // 2, kk % 2]

    def strip(i):
        left = t[:, pl.ds(pl.multiple_of(i * 256, 256), 256)]
        late = i >= 4
        g8 = 2 * i + jnp.where(late, 1, 0)
        gd = 2 * i + jnp.where(late, 0, 1)
        for j in range(5):
            jj = lax.rem(i + j, 8)
            right = t[:, pl.ds(pl.multiple_of(jj * 256, 256), 256)]
            prod = lax.dot_general(
                left, right, (((0,), (0,)), ((), ())), preferred_element_type=jnp.float32
            )
            blocks = {
                (r, c): prod[r * B : r * B + B, c * B : c * B + B] for r in range(2) for c in range(2)
            }
            for (r, c), block in blocks.items():
                if 1 <= 2 * j + c - r <= 7:
                    chunk(2 * i + r, 2 * j + c - r)[pl.ds(0, B), :] = block
            if j == 0:
                chunk(gd, 0)[pl.ds(0, B), :] = jnp.where(row <= col, blocks[0, 0], blocks[1, 1])
                chunk(gd, 0)[pl.ds(B, 1), :] = jnp.sum(
                    jnp.where(row == col, blocks[1, 1], 0.0), axis=0, keepdims=True
                )
            if j == 4:
                chunk(g8, 0)[pl.ds(0, B), :] = jnp.where(late, blocks[1, 1], blocks[0, 0])

    to_sibling = []

    def gram_rows(stage):
        z = net.hop("z", STAGES[stage])
        pl.loop(2 * z, 2 * z + 2)(strip)

    def share(stage):
        z = net.hop("z", STAGES[stage])
        to_sibling.append(net.send(p.at[z, :, :, 1 - core], d2d.at[stage], net.sibling()))

    def join(stage):
        z = net.hop("z", STAGES[stage])
        to_sibling[stage].wait_recv()

        @pl.loop(0, 4)
        def _(i):
            p[z, i, :, core] += d2d[stage, i]

        for part in parts:
            part.start(stage)

    def pass_on(stage):
        for i in (2, 0, 1):
            parts[i].pass_on(stage)
            if stage == (2 if i == 0 else 3):
                next(gather[i])

    def scores(z):
        s[pl.ds(512 * z, 512), :] = lax.dot_general(
            q[z].reshape(512, 2048),
            t[...],
            (((1,), (1,)), ((), ())),
            preferred_element_type=jnp.float32,
        )

    last = []

    def exchange(_):
        mine = p[zi, xi, yi, core, pl.ds(0, B), :] * scale
        turned = mine.T
        diagonal = p[zi, xi, yi, core, pl.ds(B, 1), :] * scale
        first = jnp.where(row <= col, mine, turned)
        second = jnp.where(row > col, mine, jnp.where(row < col, turned, jnp.broadcast_to(diagonal, (B, B))))
        even = odd == 0
        x[0] = jnp.where(packed, jnp.where(even, first, second), mine).reshape(8, 16, B)
        x[1] = jnp.where(packed, jnp.where(even, second, first), turned).reshape(8, 16, B)
        own_slot = jnp.where(packed, group, other)
        other_slot = jnp.where(packed, other, group)
        slots[own_slot] = x[0, k]
        for m in range(8):
            copy = pltpu.make_async_remote_copy(
                src_ref=x.at[1, m],
                dst_ref=slots.at[other_slot],
                send_sem=xsem.at[0, 8 + m],
                recv_sem=xsem.at[1, 8 + k],
                device_id=member(other, jnp.int32(m)),
                device_id_type=MESH,
            )
            copy.start()
            last.append(copy)
        for m in range(1, 8):
            to = lax.rem(k + m, 8)
            copy = pltpu.make_async_remote_copy(
                src_ref=x.at[0, to],
                dst_ref=slots.at[own_slot],
                send_sem=xsem.at[0, m],
                recv_sem=xsem.at[1, m],
                device_id=member(group, to),
                device_id_type=MESH,
            )
            copy.start()
            last.append(copy)

    gather = [gather_part(net, q, *part) for part in AG_PARTS]
    parts = [Reduce(net, p, bufs[i], *part) for i, part in enumerate(RS_PARTS)]
    reduce = [part.rest() for part in parts]
    def drain(kept):
        for copy in net.sent[:-kept]:
            copy.wait_send()
        del net.sent[:-kept]

    plan = {
        "drain": drain,
        "gather": lambda _: step_all(gather),
        "reduce": lambda _: step_all(reduce),
        "gram": gram_rows,
        "share": share,
        "join": join,
        "pass": pass_on,
        "scores": scores,
        "exchange": exchange,
    }

    gram_rows(0)
    gram_rows(1)
    pl.semaphore_wait(barrier, 10)
    load_q.wait()
    for step in ORDER:
        name, *at = step.split()
        plan[name](int(at[0]) if at else None)
    assert not step_all(gather) and not step_all(reduce)

    for m in range(1, 16):
        pltpu.make_async_remote_copy(
            src_ref=x.at[0, 0],
            dst_ref=slots.at[0],
            send_sem=xsem.at[0, m],
            recv_sem=xsem.at[1, m],
            device_id=net.sibling(),
            device_id_type=MESH,
        ).wait_recv()
    for c in range(16):
        g_out[:, pl.ds(c * B, B)] = slots[c]
    for copy in last + net.sent:
        copy.wait_send()


def finish(s_in, g_in, q_in, t_in, s_out, g_out, last, sem):
    done = s_in.shape[0]
    moves = [
        pltpu.make_async_copy(s_in, s_out.at[pl.ds(0, done)], sem.at[0]),
        pltpu.make_async_copy(g_in, g_out, sem.at[1]),
    ]
    for move in moves:
        move.start()
    rows = 256
    for h in range(last.shape[0] // rows):
        here = pl.ds(h * rows, rows)
        last[here, :] = lax.dot_general(
            q_in[HERE + h // 2, pl.ds(h % 2 * 2, 2)].reshape(rows, q_in.shape[-1]),
            t_in[...],
            (((1,), (1,)), ((), ())),
            preferred_element_type=jnp.float32,
        )
        move = pltpu.make_async_copy(
            last.at[here], s_out.at[pl.ds(done + h * rows, rows)], sem.at[2 + h]
        )
        move.start()
        moves.append(move)
    for move in moves:
        move.wait()


def local(scale, queries, training):
    n_rows, width = training.shape
    f32, bf16 = jnp.float32, jnp.bfloat16
    vmem, hbm = pl.BlockSpec(memory_space=pltpu.VMEM), pl.BlockSpec(memory_space=pltpu.HBM)
    scratch = [
        pltpu.VMEM((4, 4, 4, 2, CH, B), f32),
        pltpu.VMEM((4, 4, 4, CH, B), f32),
        pltpu.VMEM((2, 8, 16, B), f32),
        pltpu.VMEM((16, 16, B), f32),
    ]
    for part in RS_PARTS:
        for shapes in part_buffers(*part):
            scratch += [pltpu.VMEM(shape, f32) for shape in shapes]
    scratch += [
        pltpu.SemaphoreType.DMA((N_SEM,)),
        pltpu.SemaphoreType.DMA((N_SEM,)),
        pltpu.SemaphoreType.DMA((2, 16)),
        pltpu.SemaphoreType.DMA((6,)),
    ]
    some, gram, q, t = pl.pallas_call(
        functools.partial(kernel, scale),
        out_shape=(
            pltpu.VMEM((512 * HERE, n_rows), f32),
            pltpu.VMEM((16, 16 * B), f32),
            pltpu.VMEM((4, 4, 4, 2, 16, width), bf16),
            pltpu.VMEM((n_rows, width), bf16),
        ),
        in_specs=[hbm] * 2,
        out_specs=(vmem,) * 4,
        scratch_shapes=scratch,
        compiler_params=pltpu.CompilerParams(
            collective_id=0, has_side_effects=True, vmem_limit_bytes=24 * 2**20
        ),
        cost_estimate=pl.CostEstimate(
            flops=2 * 2048 * n_rows * 2048 * 2, bytes_accessed=20 * 2**20, transcendentals=0
        ),
    )(*(pltpu.with_memory_space_constraint(a, pltpu.HBM) for a in (queries, training)))
    return pl.pallas_call(
        finish,
        out_shape=(
            jax.ShapeDtypeStruct((2048, n_rows), f32),
            jax.ShapeDtypeStruct((16, 16 * B), f32),
        ),
        in_specs=[vmem] * 4,
        out_specs=(hbm, hbm),
        scratch_shapes=[pltpu.VMEM((512 * (4 - HERE), n_rows), f32), pltpu.SemaphoreType.DMA((10,))],
        compiler_params=pltpu.CompilerParams(vmem_limit_bytes=16 * 2**20),
    )(some, gram, q, t)


def solution(mesh):
    in_specs = (P(("blk", "grp"), None), P(("blk", "grp"), None))
    out_specs = (P(None, ("blk", "grp")), P(("blk", "grp"), None))
    return jax.shard_map(
        functools.partial(local, 1.0 / 131072),
        mesh=mesh,
        in_specs=in_specs,
        out_specs=out_specs,
        check_vma=False,
    )
```

```python
import functools

import jax
import jax.numpy as jnp
from jax import lax
from jax.experimental import pallas as pl
from jax.experimental.pallas import tpu as pltpu
from jax.sharding import PartitionSpec as P

MESH = pl.DeviceIdType.MESH
ALL = pl.ds(0, 4)
AXES = ("z", "x", "y")
B = 128
CH = 136
AG_PARTS = (((0, 640), "yxz"), ((640, 1280), "zyx"), ((1280, 2048), "xzy"))
RS_PARTS = (((0, 48), "zxy"), ((48, 96), "xyz"), ((96, 136), "yzx"))
N_SEM = 192
HERE = 3
STAGES = (2, 1, 3, 0)
ORDER = (
    "gather",
    "share 0",
    "share 1",
    "gram 2",
    "share 2",
    "join 0",
    "gather",
    "join 1",
    "gram 3",
    "share 3",
    "pass 0",
    "join 2",
    "gather",
    "pass 1",
    "join 3",
    "pass 2",
    "pass 3",
    "gather",
    "reduce",
    "gather",
    "reduce",
    "drain 30",
    "gather",
    "reduce",
    "exchange",
    "gather",
    "scores 0",
    "scores 1",
    "scores 2",
)


def stored(axis, i):
    return lax.rem(i, 2) * 2 + lax.div(i, 2) if axis == "y" else i


class Net:
    def __init__(self, ssem, rsem):
        blk, grp = lax.axis_index("blk"), lax.axis_index("grp")
        self.at = {
            "z": lax.div(blk, 8),
            "x": lax.rem(lax.div(blk, 2), 4),
            "y": lax.div(grp, 2) * 2 + lax.rem(blk, 2),
        }
        self.core = lax.rem(grp, 2)
        self.group = lax.div(blk, 2)
        self.k = lax.rem(blk, 2) * 4 + grp
        self.ssem, self.rsem = ssem, rsem
        self.count = 0
        self.sent = []

    def device(self, core=None, **moved):
        at = {**self.at, **moved}
        core = self.core if core is None else core
        return (at["z"] * 8 + at["x"] * 2 + lax.rem(at["y"], 2), lax.div(at["y"], 2) * 2 + core)

    def hop(self, axis, by):
        return lax.rem(self.at[axis] + by + 4, 4)

    def neighbour(self, axis, by):
        return self.device(**{axis: self.hop(axis, by)})

    def sibling(self):
        return self.device(core=1 - self.core)

    def send(self, src, dst, to):
        t = self.count
        self.count += 1
        copy = pltpu.make_async_remote_copy(
            src_ref=src,
            dst_ref=dst,
            send_sem=self.ssem.at[t],
            recv_sem=self.rsem.at[t],
            device_id=to,
            device_id_type=MESH,
        )
        copy.start()
        self.sent.append(copy)
        return copy


def member(group, k):
    return (group * 2 + lax.div(k, 4), lax.rem(k, 4))


def gather_part(net, q, cols, order):
    lo, hi = cols

    def region(idx, c=None):
        at = [idx[a] for a in AXES]
        return q.at[at[0], at[1], at[2], net.core, :, pl.ds(lo, hi - lo)] if c is None else q.at[
            at[0], at[1], at[2], net.core, :, pl.ds(*c)
        ]

    def halves(idx):
        free = [a for a in AXES if isinstance(idx[a], pl.Slice)]
        if free:
            return [region({**idx, free[0]: pl.ds(2 * h, 2)}) for h in range(2)]
        mid = (hi - lo) // 256 * 128
        return [region(idx, (lo, mid)), region(idx, (lo + mid, hi - lo - mid))]

    idx = {a: stored(a, net.at[a]) for a in AXES}
    to_sibling = []

    def spread(axis):
        here = region(idx)
        return [net.send(here, here, net.neighbour(axis, by)) for by in (2, 1, -1)]

    def ahead(at):
        here = region(at)
        return [net.send(here, here, net.neighbour(order[2], by)) for by in (1, -1)]

    def hand(at):
        to_sibling.append(net.send(region(at), region(at), net.sibling()))

    first = spread(order[0])
    yield
    for copy in first:
        copy.wait_recv()
    idx = {**idx, order[0]: ALL}
    axis = order[1]
    here = region(idx)
    up, down = (net.send(here, here, net.neighbour(axis, by)) for by in (1, -1))
    third = [ahead(idx)]
    hand(idx)
    yield
    up.wait_recv()
    src = halves({**idx, axis: stored(axis, net.hop(axis, -1))})[0]
    on_up = net.send(src, src, net.neighbour(axis, 1))
    down.wait_recv()
    src = halves({**idx, axis: stored(axis, net.hop(axis, 1))})[1]
    on_down = net.send(src, src, net.neighbour(axis, -1))
    yield
    on_up.wait_recv()
    on_down.wait_recv()
    for by in (1, -1, 2):
        at = {**idx, order[1]: stored(order[1], net.hop(order[1], by))}
        third.append(ahead(at))
        hand(at)
    yield
    idx = {**idx, order[1]: ALL}
    axis = order[2]
    low, high, far = ({**idx, axis: stored(axis, net.hop(axis, by))} for by in (-1, 1, 2))
    for up, _ in third:
        up.wait_recv()
    src = halves(low)[0]
    on_up = net.send(src, src, net.neighbour(axis, 1))
    for _, down in third:
        down.wait_recv()
    src = halves(high)[1]
    on_down = net.send(src, src, net.neighbour(axis, -1))
    hand(low)
    hand(high)
    yield
    on_up.wait_recv()
    on_down.wait_recv()
    hand(far)
    yield
    for copy in to_sibling:
        copy.wait_recv()


class Reduce:
    def __init__(self, net, p, bufs, rows, order):
        self.net, self.p, self.bufs, self.rows, self.order = net, p, bufs, rows, order
        self.up, self.down = net.neighbour(order[0], 1), net.neighbour(order[0], -1)
        self.copies = {}

    def region(self, idx):
        lo, hi = self.rows
        at = [idx[a] for a in AXES]
        return self.p.at[at[0], at[1], at[2], self.net.core, pl.ds(lo, hi - lo)]

    def halves(self, stage, by):
        first = self.order[0]
        if first == "z":
            idx = {"z": self.net.hop("z", by), "x": ALL, "y": ALL}
        else:
            idx = {"x": ALL, "y": ALL, "z": self.net.hop("z", STAGES[stage])}
            idx[first] = stored(first, self.net.hop(first, by))
        free = next(a for a in AXES if isinstance(idx[a], pl.Slice))
        return [self.region({**idx, free: pl.ds(2 * h, 2)}) for h in range(2)]

    def go(self, stage, name, src, slot, to):
        dst = self.bufs[0][slot]
        if self.order[0] != "z":
            dst = dst.at[stage]
        self.copies[stage, name] = self.net.send(src, dst, to), dst

    def start(self, stage):
        whole = self.order[0] != "z"
        if whole or STAGES[stage] == 2:
            far = self.halves(stage, 2)
            self.go(stage, "via_up", far[0], 0, self.up)
            self.go(stage, "via_down", far[1], 1, self.down)
        if whole or STAGES[stage] == 1:
            self.go(stage, "own_up", self.halves(stage, 1)[1], 2, self.up)
        if whole or STAGES[stage] == 3:
            self.go(stage, "own_down", self.halves(stage, -1)[0], 3, self.down)

    def add(self, ref, *arrived):
        for at in arrived:
            self.copies[at][0].wait_recv()
        total = ref[...]
        for at in arrived:
            total = total + self.copies[at][1][...]
        ref[...] = total

    def pass_on(self, stage):
        whole = self.order[0] != "z"
        via = stage if whole else STAGES.index(2)
        if whole or STAGES[stage] == 1:
            high = self.halves(stage, 1)[0]
            self.add(high, (via, "via_up"))
            self.go(stage, "sum_up", high, 4, self.up)
        if whole or STAGES[stage] == 3:
            low = self.halves(stage, -1)[1]
            self.add(low, (via, "via_down"))
            self.go(stage, "sum_down", low, 5, self.down)

    def rest(self):
        net, order = self.net, self.order
        whole = order[0] != "z"
        for stage in range(4) if whole else (None,):
            mine = self.halves(stage, 0)
            one, three = (stage, stage) if whole else (STAGES.index(1), STAGES.index(3))
            self.add(mine[1], (one, "own_up"), (three, "sum_down"))
            self.add(mine[0], (three, "own_down"), (one, "sum_up"))
        idx = {**{a: ALL for a in AXES}, order[0]: stored(order[0], net.at[order[0]])}
        for axis, buf in zip(order[1:], self.bufs[1:], strict=True):
            copies = [
                net.send(
                    self.region({**idx, axis: stored(axis, net.hop(axis, by))}),
                    buf[i],
                    net.neighbour(axis, by),
                )
                for i, by in enumerate((2, 1, -1))
            ]
            idx = {**idx, axis: stored(axis, net.at[axis])}
            yield
            for copy in copies:
                copy.wait_recv()
            self.region(idx)[...] += buf[0][...] + buf[1][...] + buf[2][...]


def part_buffers(rows, order):
    n = rows[1] - rows[0]
    return [[(2, 4, n, B) if order[0] == "z" else (4, 2, n, B)] * 6, [(4, n, B)] * 3, [(n, B)] * 3]


def step_all(gens):
    left = False
    for g in list(gens):
        try:
            next(g)
            left = True
        except StopIteration:
            gens.remove(g)
    return left


def kernel(scale, *refs):
    (q_in, t_in, s, g_out, q, t, p, d2d, x, slots) = refs[:10]
    *flat, ssem, rsem, xsem, lsem = refs[10:]
    flat = iter(flat)
    bufs = [[[next(flat) for _ in shapes] for shapes in part_buffers(*part)] for part in RS_PARTS]
    net = Net(ssem, rsem)
    zi, xi, yi = (stored(a, net.at[a]) for a in AXES)
    core, group, k = net.core, net.group, net.k
    odd = lax.rem(group, 2)
    packed = jnp.logical_and(k == 0, odd != lax.div(group, 8))
    other = jnp.where(
        packed, group + 1 - 2 * odd, lax.rem(group + jnp.where(k == 0, 8, k), 16)
    )

    load_q = pltpu.make_async_copy(q_in, q.at[zi, xi, yi, core], lsem.at[0])
    load_q.start()
    load_t = pltpu.make_async_copy(t_in, t, lsem.at[1])
    load_t.start()

    barrier = pltpu.get_barrier_semaphore()

    def greet(device):
        pl.semaphore_signal(barrier, inc=1, device_id=device, device_id_type=MESH)

    for axis in AXES:
        greet(net.neighbour(axis, 2))
    for axis in AXES:
        greet(net.neighbour(axis, 1))
        greet(net.neighbour(axis, -1))
    greet(net.sibling())
    load_t.wait()

    p[:, :, :, :, pl.ds(B, 8)] = jnp.zeros((4, 4, 4, 2, 8, B), jnp.float32)
    row = lax.broadcasted_iota(jnp.int32, (B, B), 0)
    col = lax.broadcasted_iota(jnp.int32, (B, B), 1)

    def chunk(g, kk):
        return p.at[lax.div(g, 4), lax.rem(g, 4), kk // 2, kk % 2]

    def strip(i):
        left = t[:, pl.ds(pl.multiple_of(i * 256, 256), 256)]
        late = i >= 4
        g8 = 2 * i + jnp.where(late, 1, 0)
        gd = 2 * i + jnp.where(late, 0, 1)
        for j in range(5):
            jj = lax.rem(i + j, 8)
            right = t[:, pl.ds(pl.multiple_of(jj * 256, 256), 256)]
            prod = lax.dot_general(
                left, right, (((0,), (0,)), ((), ())), preferred_element_type=jnp.float32
            )
            blocks = {
                (r, c): prod[r * B : r * B + B, c * B : c * B + B] for r in range(2) for c in range(2)
            }
            for (r, c), block in blocks.items():
                if 1 <= 2 * j + c - r <= 7:
                    chunk(2 * i + r, 2 * j + c - r)[pl.ds(0, B), :] = block
            if j == 0:
                chunk(gd, 0)[pl.ds(0, B), :] = jnp.where(row <= col, blocks[0, 0], blocks[1, 1])
                chunk(gd, 0)[pl.ds(B, 1), :] = jnp.sum(
                    jnp.where(row == col, blocks[1, 1], 0.0), axis=0, keepdims=True
                )
            if j == 4:
                chunk(g8, 0)[pl.ds(0, B), :] = jnp.where(late, blocks[1, 1], blocks[0, 0])

    to_sibling = []

    def gram_rows(stage):
        z = net.hop("z", STAGES[stage])
        pl.loop(2 * z, 2 * z + 2)(strip)

    def share(stage):
        z = net.hop("z", STAGES[stage])
        to_sibling.append(net.send(p.at[z, :, :, 1 - core], d2d.at[stage], net.sibling()))

    def join(stage):
        z = net.hop("z", STAGES[stage])
        to_sibling[stage].wait_recv()

        @pl.loop(0, 4)
        def _(i):
            p[z, i, :, core] += d2d[stage, i]

        for part in parts:
            part.start(stage)

    def pass_on(stage):
        for part in parts:
            part.pass_on(stage)

    def scores(z):
        s[pl.ds(512 * z, 512), :] = lax.dot_general(
            q[z].reshape(512, 2048),
            t[...],
            (((1,), (1,)), ((), ())),
            preferred_element_type=jnp.float32,
        )

    last = []

    def exchange(_):
        mine = p[zi, xi, yi, core, pl.ds(0, B), :] * scale
        turned = mine.T
        diagonal = p[zi, xi, yi, core, pl.ds(B, 1), :] * scale
        first = jnp.where(row <= col, mine, turned)
        second = jnp.where(row > col, mine, jnp.where(row < col, turned, jnp.broadcast_to(diagonal, (B, B))))
        even = odd == 0
        x[0] = jnp.where(packed, jnp.where(even, first, second), mine).reshape(8, 16, B)
        x[1] = jnp.where(packed, jnp.where(even, second, first), turned).reshape(8, 16, B)
        own_slot = jnp.where(packed, group, other)
        other_slot = jnp.where(packed, other, group)
        slots[own_slot] = x[0, k]
        for m in range(8):
            copy = pltpu.make_async_remote_copy(
                src_ref=x.at[1, m],
                dst_ref=slots.at[other_slot],
                send_sem=xsem.at[0, 8 + m],
                recv_sem=xsem.at[1, 8 + k],
                device_id=member(other, jnp.int32(m)),
                device_id_type=MESH,
            )
            copy.start()
            last.append(copy)
        for m in range(1, 8):
            to = lax.rem(k + m, 8)
            copy = pltpu.make_async_remote_copy(
                src_ref=x.at[0, to],
                dst_ref=slots.at[own_slot],
                send_sem=xsem.at[0, m],
                recv_sem=xsem.at[1, m],
                device_id=member(group, to),
                device_id_type=MESH,
            )
            copy.start()
            last.append(copy)

    gather = [gather_part(net, q, *part) for part in AG_PARTS]
    parts = [Reduce(net, p, bufs[i], *part) for i, part in enumerate(RS_PARTS)]
    reduce = [part.rest() for part in parts]
    def drain(kept):
        for copy in net.sent[:-kept]:
            copy.wait_send()
        del net.sent[:-kept]

    plan = {
        "drain": drain,
        "gather": lambda _: step_all(gather),
        "reduce": lambda _: step_all(reduce),
        "gram": gram_rows,
        "share": share,
        "join": join,
        "pass": pass_on,
        "scores": scores,
        "exchange": exchange,
    }

    gram_rows(0)
    gram_rows(1)
    pl.semaphore_wait(barrier, 10)
    load_q.wait()
    for step in ORDER:
        name, *at = step.split()
        plan[name](int(at[0]) if at else None)
    assert not step_all(gather) and not step_all(reduce)

    for m in range(1, 16):
        pltpu.make_async_remote_copy(
            src_ref=x.at[0, 0],
            dst_ref=slots.at[0],
            send_sem=xsem.at[0, m],
            recv_sem=xsem.at[1, m],
            device_id=net.sibling(),
            device_id_type=MESH,
        ).wait_recv()
    for c in range(16):
        g_out[:, pl.ds(c * B, B)] = slots[c]
    for copy in last + net.sent:
        copy.wait_send()


def finish(s_in, g_in, q_in, t_in, s_out, g_out, last, sem):
    done = s_in.shape[0]
    moves = [
        pltpu.make_async_copy(s_in.at[pl.ds(i * 512, 512)], s_out.at[pl.ds(i * 512, 512)], sem.at[4 + i])
        for i in range(done // 512)
    ]
    moves.append(pltpu.make_async_copy(g_in, g_out, sem.at[1]))
    for move in moves:
        move.start()
    rows = 256
    for h in range(last.shape[0] // rows):
        here = pl.ds(h * rows, rows)
        last[here, :] = lax.dot_general(
            q_in[HERE + h // 2, pl.ds(h % 2 * 2, 2)].reshape(rows, q_in.shape[-1]),
            t_in[...],
            (((1,), (1,)), ((), ())),
            preferred_element_type=jnp.float32,
        )
        move = pltpu.make_async_copy(
            last.at[here], s_out.at[pl.ds(done + h * rows, rows)], sem.at[2 + h]
        )
        move.start()
        moves.append(move)
    for move in moves:
        move.wait()


def local(scale, queries, training):
    n_rows, width = training.shape
    f32, bf16 = jnp.float32, jnp.bfloat16
    vmem, hbm = pl.BlockSpec(memory_space=pltpu.VMEM), pl.BlockSpec(memory_space=pltpu.HBM)
    scratch = [
        pltpu.VMEM((4, 4, 4, 2, CH, B), f32),
        pltpu.VMEM((4, 4, 4, CH, B), f32),
        pltpu.VMEM((2, 8, 16, B), f32),
        pltpu.VMEM((16, 16, B), f32),
    ]
    for part in RS_PARTS:
        for shapes in part_buffers(*part):
            scratch += [pltpu.VMEM(shape, f32) for shape in shapes]
    scratch += [
        pltpu.SemaphoreType.DMA((N_SEM,)),
        pltpu.SemaphoreType.DMA((N_SEM,)),
        pltpu.SemaphoreType.DMA((2, 16)),
        pltpu.SemaphoreType.DMA((6,)),
    ]
    some, gram, q, t = pl.pallas_call(
        functools.partial(kernel, scale),
        out_shape=(
            pltpu.VMEM((512 * HERE, n_rows), f32),
            pltpu.VMEM((16, 16 * B), f32),
            pltpu.VMEM((4, 4, 4, 2, 16, width), bf16),
            pltpu.VMEM((n_rows, width), bf16),
        ),
        in_specs=[hbm] * 2,
        out_specs=(vmem,) * 4,
        scratch_shapes=scratch,
        compiler_params=pltpu.CompilerParams(
            collective_id=0, has_side_effects=True, vmem_limit_bytes=24 * 2**20
        ),
        cost_estimate=pl.CostEstimate(
            flops=2 * 2048 * n_rows * 2048 * 2, bytes_accessed=20 * 2**20, transcendentals=0
        ),
    )(*(pltpu.with_memory_space_constraint(a, pltpu.HBM) for a in (queries, training)))
    return pl.pallas_call(
        finish,
        out_shape=(
            jax.ShapeDtypeStruct((2048, n_rows), f32),
            jax.ShapeDtypeStruct((16, 16 * B), f32),
        ),
        in_specs=[vmem] * 4,
        out_specs=(hbm, hbm),
        scratch_shapes=[pltpu.VMEM((512 * (4 - HERE), n_rows), f32), pltpu.SemaphoreType.DMA((16,))],
        compiler_params=pltpu.CompilerParams(vmem_limit_bytes=16 * 2**20),
    )(some, gram, q, t)


def solution(mesh):
    in_specs = (P(("blk", "grp"), None), P(("blk", "grp"), None))
    out_specs = (P(None, ("blk", "grp")), P(("blk", "grp"), None))
    return jax.shard_map(
        functools.partial(local, 1.0 / 131072),
        mesh=mesh,
        in_specs=in_specs,
        out_specs=out_specs,
        check_vma=False,
    )
```
